512 devices in a mesh: tok: 2 (over core), head: 16 (over y, x), exp: 16 (over z).
Axes of the slice: x: 4, y: 4, z: 16, core: 2. Of those that a mesh axis runs over, the one named last changes fastest.
Arguments:
- context: bfloat16 [16, 64, 4096], P('exp', 'tok', 'head'), may hold values from -6 to 6
- out_proj: bfloat16 [4096, 4096], P('head', 'exp'), may hold values from -0.125 to 0.125
- stream: float32 [16, 64, 4096], P('exp', 'tok', 'head'), may hold values from -75 to 75
- norm_gain: float32 [4096], replicated, may hold values from 0.1 to 1.9
- expert_ids: int32 [16, 64, 8], P('exp', 'tok'), may hold values from 0 to 31, as said below
- slot_ids: int32 [16, 64, 8], P('exp', 'tok'), may hold values from -1 to 11, as said below
- gate_probs: float32 [16, 64, 8], P('exp', 'tok'), may hold values from 0.02 to 0.3
- w_gate: bfloat16 [32, 3072, 4096], P(('tok', 'exp'), 'head'), may hold values from -0.09375 to 0.09375
- w_up: bfloat16 [32, 3072, 4096], P(('tok', 'exp'), 'head'), may hold values from -0.09375 to 0.09375
- w_down: bfloat16 [32, 3072, 4096], P(('tok', 'exp'), 'head'), may hold values from -0.15625 to 0.15625
Outputs:
- mixed: float32 [16, 64, 4096], P('exp', 'tok', 'head')
The draws below stay inside these ranges and needn't reach their ends.
Inputs may be any that keep to these rules, and one draw needn't show every extreme that they name: `expert_ids`: each token names 8 different experts. `slot_ids`: within a block of 32 consecutive tokens of one image, the choices of one expert take slots 0, 1, 2, ... in token order until its 12 slots are full, later ones get -1; in every block some expert fills all 12 slots.
All inputs are finite; a program needn't handle non-finite values.
Results may differ from the reference program's by a relative error of at most 0.0034.
Values may be sent and summed in bfloat16 or wider, within the bound.
No kernel may reach another device: no remote copies, remote signals or barrier semaphores. Data moves between devices by JAX's collectives and lax.ppermute only.
A program may use at most 64 MiB of HBM per device.

```python
import jax
import jax.numpy as jnp
from jax import lax

D = 4096
HID = 3072
EXPERTS = 32
TOP = 8
TOK_DEV = 32
CAP = 12
IMAGES = 16
SEQ = 64
N_HEAD = 16


def routing_table(key):
    base_key = jax.random.fold_in(key, 4242)
    key_pop, key_noise, key_hot, key_rows = jax.random.split(base_key, 4)
    block_count = IMAGES * SEQ // TOK_DEV
    popular = jax.random.randint(key_pop, (EXPERTS,), 0, 64) ** 2
    noise = jax.random.randint(key_noise, (block_count, TOK_DEV, EXPERTS), 0, 4096)
    hot_expert = jax.random.randint(key_hot, (), 0, EXPERTS)
    row_keys = jax.random.split(key_rows, block_count)
    orders = jax.vmap(lambda one_key: jax.random.permutation(one_key, TOK_DEV))(row_keys)
    places = jnp.argsort(orders, axis=1, stable=True)
    forced = (places < CAP).astype(jnp.int32)
    expert_range = jnp.arange(EXPERTS, dtype=jnp.int32)
    is_hot = (expert_range == hot_expert).astype(jnp.int32)
    score = noise + popular[None, None, :] + forced[:, :, None] * is_hot[None, None, :] * 1048576
    distinct = score * EXPERTS + expert_range[None, None, :]
    chosen = lax.top_k(distinct, TOP)[1].astype(jnp.int32)
    one_hot = jnp.sum((chosen[:, :, :, None] == expert_range).astype(jnp.int32), axis=2)
    before = jnp.cumsum(one_hot, axis=1) - one_hot
    ranked = jnp.take_along_axis(before, chosen, axis=2)
    slots = jnp.where(ranked < CAP, ranked, -1).astype(jnp.int32)
    return (chosen.reshape(IMAGES, SEQ, TOP), slots.reshape(IMAGES, SEQ, TOP))


def draw_expert_ids(key, part):
    return routing_table(key)[0]


def draw_slot_ids(key, part):
    return routing_table(key)[1]


def draw_stream(key, part):
    key_base, key_cols, key_rows = jax.random.split(jax.random.fold_in(key, 99), 3)
    col_pos = jnp.arange(D, dtype=jnp.float32) / D
    col_scale = jnp.exp(jnp.log(10.0) * col_pos) * jax.random.uniform(key_cols, (D,), jnp.float32, 0.5, 1.5)
    row_scale = jnp.exp(jnp.log(10.0) * jax.random.uniform(key_rows, (IMAGES, SEQ, 1), jnp.float32))
    values = jnp.clip(jax.random.normal(key_base, (IMAGES, SEQ, D), jnp.float32), -4.0, 4.0)
    return values * col_scale * row_scale / 8.0


def raised(drawn, key, source, target, shards_of, factor):
    owner, partner = [(jnp.arange(drawn.shape[axis_at]) // (drawn.shape[axis_at] // shards_of)).reshape([-1 if axis == axis_at else 1 for axis in range(drawn.ndim)]) for axis_at in (source, target)]
    chosen = jax.random.permutation(key, shards_of)[partner]
    strong = (owner == chosen) | (owner == (partner + shards_of // 2) % shards_of)
    return jnp.where(strong, factor * drawn, drawn)


def shard_levels(stream_key, shape, pieces, least, largest):
    factor_of, own = 1.0, jax.random.fold_in(stream_key, 6)
    for axis_at, shards_of in pieces:
        steps = jnp.exp(jax.random.uniform(jax.random.fold_in(own, axis_at), (shards_of,), jnp.float32, least / len(pieces), largest / len(pieces)))
        factor_of = factor_of * jnp.repeat(steps, shape[axis_at] // shards_of).reshape([-1 if axis == axis_at else 1 for axis in range(len(shape))])
    return factor_of


def scatter_about(own_key, shape, scale, most, cuts=(), kind=jnp.bfloat16):
    loudness = shard_levels(own_key, shape, cuts, -0.22, 0.18) if cuts else 1.0
    values = jax.random.normal(own_key, shape, jnp.float32) * scale * loudness
    return jnp.minimum(jnp.maximum(values, -most), most).astype(kind)


def gaussian_with(stream_key, extent, deviation, reach, shards, heavy, kind=jnp.bfloat16):
    drawn = deviation * jax.random.normal(stream_key, extent, jnp.float32)
    if shards:
        drawn = drawn * shard_levels(stream_key, extent, shards, -0.22, 0.18)
    return jnp.clip(raised(drawn, jax.random.fold_in(stream_key, 3), *heavy), -reach, reach).astype(kind)


def setup_inputs(seed: int = 0) -> dict:
    key_of = jax.random.split(jax.random.key(seed), 11)
    context = scatter_about(key_of[0], (IMAGES, SEQ, D), 1.0, 6.0, ((0, 16), (1, 2), (2, 16)))
    out_proj = gaussian_with(key_of[1], (D, D), D ** -0.5, 0.125, ((0, 16), (1, 16)), (0, 1, 16, 2.0))
    stream = draw_stream(jax.random.fold_in(key_of[10], 71), 0)
    norm_gain = jnp.clip(1.0 + 0.18 * jax.random.normal(key_of[3], (D,), jnp.float32), 0.1, 1.9)
    expert_ids = draw_expert_ids(jax.random.fold_in(key_of[10], 71), 0)
    slot_ids = draw_slot_ids(jax.random.fold_in(key_of[10], 71), 0)
    gate_probs = jnp.clip(0.02 + 0.28 * jax.random.uniform(key_of[6], (IMAGES, SEQ, TOP), jnp.float32) ** shard_levels(key_of[6], (IMAGES, SEQ, TOP), ((0, 16), (1, 2)), -0.2, 0.2), 0.02, 0.3)
    w_gate = scatter_about(key_of[7], (EXPERTS, HID, D), D ** -0.5, 0.09375, ((0, 32), (1, 16)))
    w_up = scatter_about(key_of[8], (EXPERTS, HID, D), D ** -0.5, 0.09375, ((0, 32), (1, 16)))
    w_down = gaussian_with(key_of[9], (EXPERTS, HID, D), HID ** -0.5, 0.15625, ((0, 32), (1, 16)), (1, 2, 16, 2.0))
    return {"context": context, "out_proj": out_proj, "stream": stream, "norm_gain": norm_gain, "expert_ids": expert_ids, "slot_ids": slot_ids, "gate_probs": gate_probs, "w_gate": w_gate, "w_up": w_up, "w_down": w_down}


eps_value = 1e-05

def reference(context, out_proj, stream, norm_gain, expert_ids, slot_ids, gate_probs, w_gate, w_up, w_down):
    token_count = IMAGES * SEQ
    block_count = token_count // TOK_DEV
    flat_context = context.reshape(token_count, D)
    resid_mid = stream.reshape(token_count, D) + jnp.dot(flat_context, out_proj, preferred_element_type=jnp.float32)
    mean_sq = lax.optimization_barrier(jnp.mean(resid_mid * resid_mid, axis=1, keepdims=True))
    normed = (resid_mid * lax.rsqrt(mean_sq + eps_value) * norm_gain).astype(jnp.bfloat16)
    choice_ids = expert_ids.reshape(token_count, TOP).astype(jnp.int32)
    choice_slots = slot_ids.reshape(token_count, TOP).astype(jnp.int32)
    weights = gate_probs.reshape(token_count, TOP)
    block_of = (jnp.arange(token_count, dtype=jnp.int32) // TOK_DEV)[:, None]
    spill_slot = EXPERTS * block_count * CAP
    target = jnp.where(choice_slots >= 0, (choice_ids * block_count + block_of) * CAP + choice_slots, spill_slot).astype(jnp.int32)
    buffer_rows = jnp.zeros((spill_slot + 1, D), jnp.bfloat16).at[target.reshape(-1)].set(jnp.repeat(normed, TOP, axis=0))
    dispatched = buffer_rows[:spill_slot].reshape(EXPERTS, block_count * CAP, D)

    def expert_hidden(operands):
        inputs, gate_mat, up_mat = operands
        gate_part = jnp.dot(inputs, gate_mat.T, preferred_element_type=jnp.float32)
        up_part = jnp.dot(inputs, up_mat.T, preferred_element_type=jnp.float32)
        return (jax.nn.silu(gate_part) * up_part).astype(jnp.bfloat16)
    hidden = lax.map(expert_hidden, (dispatched, w_gate, w_up))
    slice_width = HID // N_HEAD

    def add_slice(index, total):
        first = index * slice_width
        hidden_slice = lax.dynamic_slice_in_dim(hidden, first, slice_width, 2).astype(jnp.float32)
        down_slice = lax.dynamic_slice_in_dim(w_down, first, slice_width, 1).astype(jnp.float32)
        part = jnp.einsum('erh,ehd->erd', hidden_slice, down_slice, precision=lax.Precision.HIGHEST).astype(jnp.bfloat16)
        lookup = jnp.concatenate([part.reshape(spill_slot, D), jnp.zeros((1, D), jnp.bfloat16)], axis=0)
        picked = lookup[target]
        return total + lax.optimization_barrier(jnp.sum(picked.astype(jnp.float32) * weights[:, :, None], axis=1))
    expert_mix = lax.fori_loop(0, N_HEAD, add_slice, jnp.zeros((token_count, D), jnp.float32))
    return (resid_mid + expert_mix).reshape(IMAGES, SEQ, D)
```

```python
import functools

import jax
import jax.numpy as jnp
import numpy as np
from jax import lax
from jax.experimental import pallas as pl
from jax.experimental.pallas import tpu as pltpu
from jax.sharding import Mesh
from jax.sharding import PartitionSpec as P

CAP = 12
TOK = 32
COLS = 256
GRID_Y = 4
GRID_X = 4
HEADS = 16
EXPS = 16
WIDTH = HEADS * COLS
HALF = WIDTH // 2
ROWS = 2 * EXPS * CAP
HEAD = ("head_0", "head_1")
EPS = 1e-05
BF16 = jnp.bfloat16
F32 = jnp.float32

VMEM = pl.BlockSpec(memory_space=pltpu.VMEM)
SMEM = pl.BlockSpec(memory_space=pltpu.SMEM)


def call(kernel, out_shape, scalars, arrays, flops=0, moved=0):
    return pl.pallas_call(
        kernel,
        out_shape=out_shape,
        in_specs=[SMEM] * len(scalars) + [VMEM] * len(arrays),
        out_specs=jax.tree.map(lambda _: VMEM, out_shape),
        compiler_params=pltpu.CompilerParams(vmem_limit_bytes=48 * 1024 * 1024),
        cost_estimate=pl.CostEstimate(flops=flops, bytes_accessed=moved, transcendentals=0),
    )(*scalars, *arrays)


def shape_of(*dims, dtype=BF16):
    return jax.ShapeDtypeStruct(dims, dtype)


def exchange(x, axes):
    return lax.all_to_all(x, axes, split_axis=0, concat_axis=0, tiled=True)


def project_kernel(head_ref, got_ref, weight_ref, partial_ref, routes_ref):
    rows = got_ref[:, 0:TOK, :].reshape(EXPS * TOK, COLS)
    product = jnp.dot(rows, weight_ref[...], preferred_element_type=F32)
    partial_ref[...] = product.astype(BF16).reshape(EXPS, TOK, COLS)
    routes_ref[...] = got_ref[head_ref[0], TOK : TOK + 16, :].astype(F32)


def residual_kernel(parts_ref, stream_ref, resid_ref, copies_ref):
    total = parts_ref[0].astype(F32)
    for index in range(1, HEADS):
        total = total + parts_ref[index].astype(F32)
    total = total + stream_ref[...]
    resid_ref[...] = total
    rounded = total.astype(BF16)
    for index in range(EXPS):
        copies_ref[index] = rounded


def dispatch_kernel(exp_ref, rows_ref, routes_ref, gain_ref, out_ref):
    squares = jnp.zeros((TOK, COLS), F32)
    for block in range(EXPS):
        value = rows_ref[block].astype(F32)
        squares = squares + value * value
    scale = lax.rsqrt(jnp.sum(squares, axis=1, keepdims=True) / WIDTH + EPS)
    ids = routes_ref[0:8, 0 : 2 * TOK]
    slots = routes_ref[8:16, 0 : 2 * TOK]
    here = exp_ref[0].astype(F32)
    taken = []
    for core in range(2):
        match = ids == here + float(core * EXPS)
        taken.append(jnp.sum(jnp.where(match, slots + 1.0, 0.0), axis=0, keepdims=True) - 1.0)
    row = lax.broadcasted_iota(jnp.int32, (4 * CAP, 2 * TOK), 0)
    col = lax.broadcasted_iota(jnp.int32, (4 * CAP, 2 * TOK), 1)
    second = row >= 2 * CAP
    row_in = jnp.where(second, row - 2 * CAP, row)
    upper = row_in >= CAP
    slot = jnp.where(upper, row_in - CAP, row_in).astype(F32)
    same_half = upper == (col >= TOK)
    wanted = jnp.where(second, taken[1], taken[0])
    select = jnp.where((wanted == slot) & same_half, 1.0, 0.0).astype(BF16)
    for block in range(EXPS // 2):
        pair = []
        for piece in (block, block + EXPS // 2):
            gain = gain_ref[0:1, piece * COLS : (piece + 1) * COLS]
            pair.append((rows_ref[piece].astype(F32) * scale * gain).astype(BF16))
        picked = jnp.dot(select, jnp.concatenate(pair, axis=0), preferred_element_type=F32)
        picked = picked.astype(BF16)
        for head in range(HEADS):
            out_ref[head, :, block * COLS : (block + 1) * COLS] = picked


def hidden_kernel(rows_ref, gate_ref, up_ref, order_ref, out_ref):
    contract = (((1,), (1,)), ((), ()))

    def both_halves(weight_ref):
        low = lax.dot_general(
            weight_ref[:, :HALF], rows_ref[...], contract, preferred_element_type=F32
        )
        high = lax.dot_general(
            weight_ref[:, HALF:], rows_ref[...], contract, preferred_element_type=F32
        )
        return low + pltpu.roll(high, high.shape[1] - CAP, 1)

    gate = both_halves(gate_ref)
    up = both_halves(up_ref)
    hidden = (gate / (1.0 + jnp.exp(-gate)) * up).astype(BF16)
    ordered = jnp.dot(hidden, order_ref[...], preferred_element_type=F32).astype(BF16)
    for index in range(GRID_X):
        out_ref[index] = ordered


def pieces_kernel(x_ref, weight_ref, *out_refs):
    for step, out_ref in enumerate(out_refs):
        column = lax.rem(x_ref[0] + step, GRID_X)
        for row in range(GRID_Y):
            start = pl.multiple_of((row * GRID_X + column) * COLS, COLS)
            out_ref[:, row * COLS : (row + 1) * COLS] = weight_ref[:, pl.ds(start, COLS)]


def down_kernel(x_ref, hidden_ref, *refs):
    weights, out_ref = refs[:-1], refs[-1]
    contract = (((0,), (0,)), ((), ()))
    total = jnp.zeros((ROWS, GRID_Y * COLS), F32)
    for step, weight_ref in enumerate(weights):
        source = lax.rem(x_ref[0] + GRID_X - step, GRID_X)
        total = total + lax.dot_general(
            hidden_ref[source], weight_ref[...], contract, preferred_element_type=F32
        )
    rounded = total.astype(BF16)
    for half in range(2):
        for row in range(GRID_Y):
            out_ref[half * GRID_Y + row] = rounded[
                half * EXPS * CAP : (half + 1) * EXPS * CAP, row * COLS : (row + 1) * COLS
            ]


def collect_kernel(parts_ref, order_ref, out_ref):
    halves = []
    for core in range(2):
        total = parts_ref[core * GRID_Y].astype(F32)
        for row in range(1, GRID_Y):
            total = total + parts_ref[core * GRID_Y + row].astype(F32)
        halves.append(total.astype(BF16))
    stacked = jnp.concatenate(halves, axis=0)
    out_ref[...] = jnp.dot(order_ref[...], stacked, preferred_element_type=F32).astype(BF16)


def mix_kernel(results_ref, target_ref, probs_ref, resid_ref, out_ref):
    place = lax.broadcasted_iota(jnp.int32, (TOK, ROWS), 1)
    weights = jnp.zeros((TOK, ROWS), F32)
    for choice in range(8):
        hit = place == target_ref[:, choice : choice + 1]
        weights = weights + jnp.where(hit, probs_ref[:, choice : choice + 1], 0.0)
    coarse = weights.astype(BF16)
    fine = (weights - coarse.astype(F32)).astype(BF16)
    results = results_ref[...]
    mixed = jnp.dot(coarse, results, preferred_element_type=F32)
    mixed = mixed + jnp.dot(fine, results, preferred_element_type=F32)
    out_ref[...] = resid_ref[...] + mixed


def slot_order():
    order = np.zeros((2 * ROWS, ROWS), np.float32)
    for image in range(EXPS):
        for half in range(2):
            for slot in range(CAP):
                order[(image * 2 + half) * 2 * CAP + slot, (half * EXPS + image) * CAP + slot] = 1
    return order


def return_order():
    order = np.zeros((ROWS, ROWS), np.float32)
    for image in range(EXPS):
        for core in range(2):
            for slot in range(CAP):
                order[(image * 2 + core) * CAP + slot, (core * EXPS + image) * CAP + slot] = 1
    return order


def on_device(
    context, out_proj, stream, norm_gain, expert_ids, slot_ids, gate_probs, w_gate, w_up, w_down
):
    head = lax.axis_index(HEAD).astype(jnp.int32)[None]
    exp = lax.axis_index("exp").astype(jnp.int32)[None]
    x_at = lax.axis_index("head_1").astype(jnp.int32)[None]
    turn = [(a * EXPS + b, b * EXPS + a) for a in range(HEADS) for b in range(EXPS)]
    turned = HEAD + ("exp",)

    ids, slots = expert_ids[0], slot_ids[0]
    routes = jnp.concatenate([ids.T, slots.T], axis=0).astype(BF16)
    routes = jnp.pad(jnp.concatenate([routes, routes], axis=1), ((0, 0), (0, COLS - 2 * TOK)))
    payload = jnp.concatenate([context[0], routes], axis=0)
    got = exchange(jnp.broadcast_to(payload, (EXPS, *payload.shape)), "exp")

    stream_turned = lax.ppermute(stream[0], turned, turn)
    downs = call(
        pieces_kernel, [shape_of(192, GRID_Y * COLS)] * GRID_X, [x_at], [w_down[0]], moved=3 << 20
    )
    down_parts = [downs[0]]
    for step in range(1, GRID_X):
        ring = [(a, (a + step) % GRID_X) for a in range(GRID_X)]
        down_parts.append(lax.ppermute(downs[step], "head_1", ring))

    partial, routed = call(
        project_kernel,
        (shape_of(EXPS, TOK, COLS), shape_of(16, COLS, dtype=F32)),
        [head],
        [got, out_proj],
    )
    parts = exchange(partial, HEAD)
    resid_turned, copies = call(
        residual_kernel,
        (shape_of(TOK, COLS, dtype=F32), shape_of(EXPS, TOK, COLS)),
        [],
        [parts, stream_turned],
    )
    resid = lax.ppermute(resid_turned, turned, turn)
    rows = exchange(copies, "exp")
    rows, *down_parts = lax.optimization_barrier((rows, *down_parts))
    outgoing = call(
        dispatch_kernel,
        shape_of(HEADS, 4 * CAP, HALF),
        [exp],
        [rows, routed, norm_gain.reshape(1, WIDTH)],
    )
    arrived = exchange(outgoing.reshape(2 * HEADS, 2 * CAP, HALF), HEAD + ("tok",))
    hidden = call(
        hidden_kernel,
        shape_of(GRID_X, 192, ROWS),
        [],
        [arrived.reshape(2 * ROWS, HALF), w_gate[0], w_up[0], jnp.asarray(slot_order(), BF16)],
    )
    hidden_row = exchange(hidden, "head_1")
    produced = call(
        down_kernel, shape_of(2 * GRID_Y, ROWS // 2, COLS), [x_at], [hidden_row, *down_parts]
    )
    gathered = exchange(produced, ("tok", "head_0"))
    summed = call(
        collect_kernel,
        shape_of(ROWS, COLS),
        [],
        [gathered, jnp.asarray(return_order(), BF16)],
    )
    results = exchange(summed.reshape(EXPS, 2 * CAP, COLS), "exp")
    core = ids // EXPS
    target = jnp.where(slots >= 0, ((ids - core * EXPS) * 2 + core) * CAP + slots, -1)
    mixed = call(
        mix_kernel,
        shape_of(TOK, COLS, dtype=F32),
        [],
        [results.reshape(ROWS, COLS), target, gate_probs[0], resid],
    )
    return mixed[None]


def solution(mesh):
    split = Mesh(
        mesh.devices.reshape(mesh.shape["tok"], GRID_Y, GRID_X, mesh.shape["exp"]),
        ("tok", "head_0", "head_1", "exp"),
    )
    in_specs = (
        P("exp", "tok", HEAD),
        P(HEAD, "exp"),
        P("exp", "tok", HEAD),
        P(),
        P("exp", "tok", None),
        P("exp", "tok", None),
        P("exp", "tok", None),
        P(("tok", "exp"), HEAD, None),
        P(("tok", "exp"), HEAD, None),
        P(("tok", "exp"), HEAD, None),
    )
    return jax.shard_map(
        on_device,
        mesh=split,
        in_specs=in_specs,
        out_specs=P("exp", "tok", HEAD),
        check_vma=False,
    )
```

```python
import jax
import jax.numpy as jnp
import numpy as np
from jax import lax
from jax.experimental import pallas as pl
from jax.experimental.pallas import tpu as pltpu
from jax.sharding import Mesh
from jax.sharding import PartitionSpec as P

CAP = 12
LINE = 4
GROUP = LINE * CAP
TOK = 32
COLS = 256
HEADS = 16
EXPS = 16
WIDTH = HEADS * COLS
ROWS = 2 * EXPS * CAP
HEAD = ("head_0", "head_1")
PLANE = ("tok", "head_0", "head_1")
EPS = 1e-05
BF16 = jnp.bfloat16
F32 = jnp.float32

VMEM = pl.BlockSpec(memory_space=pltpu.VMEM)
SMEM = pl.BlockSpec(memory_space=pltpu.SMEM)


def call(kernel, out_shape, scalars, arrays, flops=0, moved=0):
    return pl.pallas_call(
        kernel,
        out_shape=out_shape,
        in_specs=[SMEM] * len(scalars) + [VMEM] * len(arrays),
        out_specs=jax.tree.map(lambda _: VMEM, out_shape),
        compiler_params=pltpu.CompilerParams(vmem_limit_bytes=48 * 1024 * 1024),
        cost_estimate=pl.CostEstimate(flops=flops, bytes_accessed=moved, transcendentals=0),
    )(*scalars, *arrays)


def shape_of(*dims, dtype=BF16):
    return jax.ShapeDtypeStruct(dims, dtype)


def exchange(x, axes):
    return lax.all_to_all(x, axes, split_axis=0, concat_axis=0, tiled=True)


def project_kernel(rows_ref, weight_ref, partial_ref):
    partial_ref[...] = jnp.dot(
        rows_ref[...], weight_ref[...], preferred_element_type=F32
    ).astype(BF16)


def residual_kernel(parts_ref, turned_ref, resid_ref, slots_ref):
    total = parts_ref[0].astype(F32)
    for index in range(1, HEADS):
        total = total + parts_ref[index].astype(F32)
    total = total + turned_ref[0:TOK, :]
    resid_ref[...] = total
    place = lax.broadcasted_iota(jnp.int32, (ROWS, TOK), 0).astype(F32)
    select = jnp.zeros((ROWS, TOK), F32)
    for choice in range(8):
        wanted = turned_ref[TOK + choice : TOK + choice + 1, 0:TOK]
        select = jnp.where(place == wanted, 1.0, select)
    picked = jnp.dot(select.astype(BF16), total.astype(BF16), preferred_element_type=F32)
    slots_ref[...] = picked.astype(BF16)


def norm_kernel(rows_ref, gain_ref, out_ref):
    squares = jnp.zeros((2 * CAP, COLS), F32)
    for block in range(EXPS):
        value = rows_ref[block].astype(F32)
        squares = squares + value * value
    scale = lax.rsqrt(jnp.sum(squares, axis=1, keepdims=True) / WIDTH + EPS)
    for block in range(EXPS):
        at = slice(block * COLS, (block + 1) * COLS)
        value = (rows_ref[block].astype(F32) * scale * gain_ref[0:1, at]).astype(BF16)
        for peer in range(LINE):
            out_ref[peer, :, at] = value


def forward_kernel(core_ref, rows_ref, order_ref, out_ref):
    order = order_ref[core_ref[0]]
    for block in range(HEADS):
        at = slice(block * COLS, (block + 1) * COLS)
        value = jnp.dot(order, rows_ref[:, at], preferred_element_type=F32).astype(BF16)
        for peer in range(LINE):
            out_ref[peer, :, at] = value


def expert_kernel(core_ref, rows_ref, *refs):
    weights, out_ref = refs[:-1], refs[-1]
    contract = (((1,), (1,)), ((), ()))
    hidden = []
    for number in range(2):
        gate_ref, up_ref = weights[number], weights[2 + number]
        rows = rows_ref[:, number * GROUP : (number + 1) * GROUP, :].reshape(LINE * GROUP, WIDTH)
        gate = lax.dot_general(rows, gate_ref[...], contract, preferred_element_type=F32)
        up = lax.dot_general(rows, up_ref[...], contract, preferred_element_type=F32)
        hidden.append((gate / (1.0 + jnp.exp(-gate)) * up).astype(BF16))
    first = core_ref[0] == 0
    for peer in range(LINE):
        for sub in range(LINE):
            block = jnp.where(first, sub * LINE + peer, peer * LINE + sub)
            at = pl.ds(pl.multiple_of(block * COLS, COLS), COLS)
            for number in range(2):
                value = jnp.dot(
                    hidden[number], weights[4 + number][:, at], preferred_element_type=F32
                )
                out_ref[peer, sub * 2 + number] = value.astype(BF16)


def add_kernel(parts_ref, out_ref):
    for index in range(2 * LINE):
        total = parts_ref[0, index].astype(F32)
        for source in range(1, LINE):
            total = total + parts_ref[source, index].astype(F32)
        out_ref[index] = total.astype(BF16)


def collect_kernel(core_ref, parts_ref, order_ref, out_ref):
    total = parts_ref[0].astype(F32)
    for source in range(1, LINE):
        total = total + parts_ref[source].astype(F32)
    order = order_ref[core_ref[0]]
    out_ref[...] = jnp.dot(order, total.astype(BF16), preferred_element_type=F32).astype(BF16)


def mix_kernel(results_ref, target_ref, probs_ref, resid_ref, out_ref):
    place = lax.broadcasted_iota(jnp.int32, (TOK, ROWS), 1)
    weights = jnp.zeros((TOK, ROWS), F32)
    for choice in range(8):
        hit = place == target_ref[:, choice : choice + 1]
        weights = weights + jnp.where(hit, probs_ref[:, choice : choice + 1], 0.0)
    coarse = weights.astype(BF16)
    fine = (weights - coarse.astype(F32)).astype(BF16)
    results = results_ref[...]
    mixed = jnp.dot(coarse, results, preferred_element_type=F32)
    mixed = mixed + jnp.dot(fine, results, preferred_element_type=F32)
    out_ref[...] = resid_ref[...] + mixed


def forward_order():
    order = np.zeros((2, 2 * GROUP, 2 * GROUP), np.float32)
    for core in range(2):
        for number in range(2):
            for inner in range(LINE):
                for slot in range(CAP):
                    source = (inner * 2 + (core ^ number)) * CAP + slot
                    order[core, (number * LINE + inner) * CAP + slot, source] = 1
    return jnp.asarray(order, BF16)


def return_order():
    order = np.zeros((2, ROWS, ROWS), np.float32)
    for core in range(2):
        for number in range(2):
            for outer in range(LINE):
                for inner in range(LINE):
                    image = outer * LINE + inner if core == 0 else inner * LINE + outer
                    for slot in range(CAP):
                        source = ((number * LINE + outer) * LINE + inner) * CAP + slot
                        order[core, (image * 2 + (core ^ number)) * CAP + slot, source] = 1
    return jnp.asarray(order, BF16)


def plane_lines():
    lines_x = [[[(t * LINE + y) * LINE + x for x in range(LINE)] for y in range(LINE)] for t in (0, 1)]
    lines_y = [[[(t * LINE + y) * LINE + x for y in range(LINE)] for x in range(LINE)] for t in (0, 1)]
    return lines_x[0] + lines_y[1], lines_y[0] + lines_x[1]


def exchange_lines(x, lines):
    return lax.all_to_all(
        x, PLANE, split_axis=0, concat_axis=0, tiled=True, axis_index_groups=lines
    )


def on_device(
    context, out_proj, stream, norm_gain, expert_ids, slot_ids, gate_probs, w_gate, w_up, w_down
):
    core = lax.axis_index("tok").astype(jnp.int32)[None]
    turn = [(a * EXPS + b, b * EXPS + a) for a in range(HEADS) for b in range(EXPS)]
    turned = HEAD + ("exp",)
    first_lines, second_lines = plane_lines()

    got = exchange(jnp.broadcast_to(context[0], (EXPS, TOK, COLS)), "exp")

    ids, slots = expert_ids[0], slot_ids[0]
    owner = ids // EXPS
    target = jnp.where(slots >= 0, ((ids - owner * EXPS) * 2 + owner) * CAP + slots, -1)
    routes = jnp.pad(target.T.astype(F32), ((0, 0), (0, COLS - TOK)))
    stream_turned = lax.ppermute(jnp.concatenate([stream[0], routes], axis=0), turned, turn)
    got, stream_turned = lax.optimization_barrier((got, stream_turned))

    partial = call(
        project_kernel, shape_of(EXPS * TOK, COLS), [], [got.reshape(EXPS * TOK, COLS), out_proj]
    )
    parts = exchange(partial.reshape(HEADS, TOK, COLS), HEAD)
    resid_turned, picked = call(
        residual_kernel,
        (shape_of(TOK, COLS, dtype=F32), shape_of(ROWS, COLS)),
        [],
        [parts, stream_turned],
    )
    resid = lax.ppermute(resid_turned, turned, turn)
    weights = []
    for weight in (w_gate[0], w_up[0], w_down[0]):
        weights += [weight, lax.ppermute(weight, "tok", [(0, 1), (1, 0)])]
    rows = exchange(picked.reshape(EXPS, 2 * CAP, COLS), "exp")
    rows, *weights = lax.optimization_barrier((rows, *weights))
    normed = call(
        norm_kernel,
        shape_of(LINE, 2 * CAP, WIDTH),
        [],
        [rows, norm_gain.reshape(1, WIDTH)],
    )
    line = exchange_lines(normed, first_lines)
    forward = call(
        forward_kernel,
        shape_of(LINE, 2 * GROUP, WIDTH),
        [core],
        [line.reshape(2 * GROUP, WIDTH), forward_order()],
    )
    arrived = exchange_lines(forward, second_lines)
    arrived, resid = lax.optimization_barrier((arrived, resid))
    produced = call(
        expert_kernel,
        shape_of(LINE, 2 * LINE, LINE * GROUP, COLS),
        [core],
        [arrived, *weights],
    )
    summed = call(
        add_kernel,
        shape_of(2 * LINE, LINE * GROUP, COLS),
        [],
        [exchange_lines(produced, first_lines)],
    )
    collected = call(
        collect_kernel,
        shape_of(ROWS, COLS),
        [core],
        [exchange_lines(summed.reshape(LINE, ROWS, COLS), second_lines), return_order()],
    )
    results = exchange(collected.reshape(EXPS, 2 * CAP, COLS), "exp")
    mixed = call(
        mix_kernel,
        shape_of(TOK, COLS, dtype=F32),
        [],
        [results.reshape(ROWS, COLS), target, gate_probs[0], resid],
    )
    return mixed[None]


def solution(mesh):
    split = Mesh(
        mesh.devices.reshape(mesh.shape["tok"], LINE, LINE, mesh.shape["exp"]),
        ("tok", "head_0", "head_1", "exp"),
    )
    in_specs = (
        P("exp", "tok", HEAD),
        P(HEAD, "exp"),
        P("exp", "tok", HEAD),
        P(),
        P("exp", "tok", None),
        P("exp", "tok", None),
        P("exp", "tok", None),
        P(("tok", "exp"), HEAD, None),
        P(("tok", "exp"), HEAD, None),
        P(("tok", "exp"), HEAD, None),
    )
    return jax.shard_map(
        on_device,
        mesh=split,
        in_specs=in_specs,
        out_specs=P("exp", "tok", HEAD),
        check_vma=False,
    )
```

```python
import jax
import jax.numpy as jnp
import numpy as np
from jax import lax
from jax.experimental import pallas as pl
from jax.experimental.pallas import tpu as pltpu
from jax.sharding import Mesh
from jax.sharding import PartitionSpec as P

CAP = 12
LINE = 4
UNITS = 192
GROUP = LINE * CAP
TOK = 32
COLS = 256
HEADS = 16
EXPS = 16
WIDTH = HEADS * COLS
ROWS = 2 * EXPS * CAP
HEAD = ("head_0", "head_1")
PLANE = ("tok", "head_0", "head_1")
EPS = 1e-05
BF16 = jnp.bfloat16
F32 = jnp.float32

VMEM = pl.BlockSpec(memory_space=pltpu.VMEM)
HBM = pl.BlockSpec(memory_space=pltpu.HBM)
SMEM = pl.BlockSpec(memory_space=pltpu.SMEM)


def call(kernel, out_shape, scalars, arrays, mib=12):
    return pl.pallas_call(
        kernel,
        out_shape=out_shape,
        in_specs=[SMEM] * len(scalars) + [VMEM] * len(arrays),
        out_specs=jax.tree.map(lambda _: VMEM, out_shape),
        compiler_params=pltpu.CompilerParams(vmem_limit_bytes=mib << 20),
    )(*scalars, *arrays)


def shape_of(*dims, dtype=BF16):
    return jax.ShapeDtypeStruct(dims, dtype)


def exchange(x, axes):
    return lax.all_to_all(x, axes, split_axis=0, concat_axis=0, tiled=True)


def project_kernel(rows_ref, weight_ref, partial_ref):
    partial_ref[...] = jnp.dot(
        rows_ref[...], weight_ref[...], preferred_element_type=F32
    ).astype(BF16)


def residual_kernel(parts_ref, turned_ref, resid_ref, slots_ref):
    total = parts_ref[0].astype(F32)
    for index in range(1, HEADS):
        total = total + parts_ref[index].astype(F32)
    total = total + turned_ref[0:TOK, :]
    resid_ref[...] = total
    place = lax.broadcasted_iota(jnp.int32, (ROWS, TOK), 0).astype(F32)
    select = jnp.zeros((ROWS, TOK), F32)
    for choice in range(8):
        wanted = turned_ref[TOK + choice : TOK + choice + 1, 0:TOK]
        select = jnp.where(place == wanted, 1.0, select)
    picked = jnp.dot(select.astype(BF16), total.astype(BF16), preferred_element_type=F32)
    slots_ref[...] = picked.astype(BF16)


def norm_kernel(rows_ref, gain_ref, out_ref):
    squares = jnp.zeros((2 * CAP, COLS), F32)
    for block in range(EXPS):
        value = rows_ref[block].astype(F32)
        squares = squares + value * value
    scale = lax.rsqrt(jnp.sum(squares, axis=1, keepdims=True) / WIDTH + EPS)
    for block in range(EXPS):
        at = slice(block * COLS, (block + 1) * COLS)
        value = (rows_ref[block].astype(F32) * scale * gain_ref[0:1, at]).astype(BF16)
        for peer in range(LINE):
            out_ref[peer, :, at] = value


def forward_kernel(core_ref, rows_ref, order_ref, out_ref):
    order = order_ref[core_ref[0]]
    for block in range(HEADS):
        at = slice(block * COLS, (block + 1) * COLS)
        value = jnp.dot(order, rows_ref[:, at], preferred_element_type=F32).astype(BF16)
        for peer in range(LINE):
            out_ref[peer, :, at] = value


def expert_kernel(core_ref, rows_ref, *refs):
    sources, out_ref, rows_held, held, staged, sems = refs[:6], *refs[6:]

    def load_rows(number):
        copies = []
        for source in range(LINE):
            at = pl.ds(number * GROUP, GROUP)
            to = pl.ds(source * GROUP, GROUP)
            sem = sems.at[6 + LINE + number * LINE + source]
            copies.append(
                pltpu.make_async_copy(rows_ref.at[source, at], rows_held.at[number, to], sem)
            )
            copies[-1].start()
        return copies

    def load(index):
        copy = pltpu.make_async_copy(sources[index], held.at[index], sems.at[index])
        copy.start()
        return copy

    rows_copies, gates, ups = [], [], []
    for number in range(2):
        rows_copies.append(load_rows(number))
        gates.append(load(number))
        ups.append(load(2 + number))
    downs = [load(4), load(5)]
    contract = (((1,), (1,)), ((), ()))
    hidden = []
    for number in range(2):
        for copy in rows_copies[number]:
            copy.wait()
        gates[number].wait()
        rows = rows_held[number]
        gate = lax.dot_general(rows, held[number], contract, preferred_element_type=F32)
        ups[number].wait()
        up = lax.dot_general(rows, held[2 + number], contract, preferred_element_type=F32)
        hidden.append((gate / (1.0 + jnp.exp(-gate)) * up).astype(BF16))
    for copy in downs:
        copy.wait()
    first = core_ref[0] == 0
    writes = []
    for peer in range(LINE):
        for sub in range(LINE):
            block = jnp.where(first, sub * LINE + peer, peer * LINE + sub)
            at = pl.ds(pl.multiple_of(block * COLS, COLS), COLS)
            for number in range(2):
                value = jnp.dot(hidden[number], held[4 + number, :, at], preferred_element_type=F32)
                staged[peer, sub * 2 + number] = value.astype(BF16)
        write = pltpu.make_async_copy(staged.at[peer], out_ref.at[peer], sems.at[6 + peer])
        write.start()
        writes.append(write)
    for write in writes:
        write.wait()


def add_kernel(parts_ref, out_ref):
    for index in range(2 * LINE):
        total = parts_ref[0, index].astype(F32)
        for source in range(1, LINE):
            total = total + parts_ref[source, index].astype(F32)
        out_ref[index] = total.astype(BF16)


def collect_kernel(core_ref, parts_ref, order_ref, out_ref):
    total = parts_ref[0].astype(F32)
    for source in range(1, LINE):
        total = total + parts_ref[source].astype(F32)
    order = order_ref[core_ref[0]]
    out_ref[...] = jnp.dot(order, total.astype(BF16), preferred_element_type=F32).astype(BF16)


def mix_kernel(results_ref, target_ref, probs_ref, resid_ref, out_ref):
    place = lax.broadcasted_iota(jnp.int32, (TOK, ROWS), 1)
    weights = jnp.zeros((TOK, ROWS), F32)
    for choice in range(8):
        hit = place == target_ref[:, choice : choice + 1]
        weights = weights + jnp.where(hit, probs_ref[:, choice : choice + 1], 0.0)
    coarse = weights.astype(BF16)
    fine = (weights - coarse.astype(F32)).astype(BF16)
    results = results_ref[...]
    mixed = jnp.dot(coarse, results, preferred_element_type=F32)
    mixed = mixed + jnp.dot(fine, results, preferred_element_type=F32)
    out_ref[...] = resid_ref[...] + mixed


def forward_order():
    order = np.zeros((2, 2 * GROUP, 2 * GROUP), np.float32)
    for core in range(2):
        for number in range(2):
            for inner in range(LINE):
                for slot in range(CAP):
                    source = (inner * 2 + (core ^ number)) * CAP + slot
                    order[core, (number * LINE + inner) * CAP + slot, source] = 1
    return jnp.asarray(order, BF16)


def return_order():
    order = np.zeros((2, ROWS, ROWS), np.float32)
    for core in range(2):
        for number in range(2):
            for outer in range(LINE):
                for inner in range(LINE):
                    image = outer * LINE + inner if core == 0 else inner * LINE + outer
                    for slot in range(CAP):
                        source = ((number * LINE + outer) * LINE + inner) * CAP + slot
                        order[core, (image * 2 + (core ^ number)) * CAP + slot, source] = 1
    return jnp.asarray(order, BF16)


def plane_lines():
    lines_x = [[[(t * LINE + y) * LINE + x for x in range(LINE)] for y in range(LINE)] for t in (0, 1)]
    lines_y = [[[(t * LINE + y) * LINE + x for y in range(LINE)] for x in range(LINE)] for t in (0, 1)]
    return lines_x[0] + lines_y[1], lines_y[0] + lines_x[1]


def exchange_lines(x, lines):
    return lax.all_to_all(
        x, PLANE, split_axis=0, concat_axis=0, tiled=True, axis_index_groups=lines
    )


def on_device(
    context, out_proj, stream, norm_gain, expert_ids, slot_ids, gate_probs, w_gate, w_up, w_down
):
    core = lax.axis_index("tok").astype(jnp.int32)[None]
    turn = [(a * EXPS + b, b * EXPS + a) for a in range(HEADS) for b in range(EXPS)]
    turned = HEAD + ("exp",)
    first_lines, second_lines = plane_lines()

    got = exchange(jnp.broadcast_to(context[0], (EXPS, TOK, COLS)), "exp")

    ids, slots = expert_ids[0], slot_ids[0]
    owner = ids // EXPS
    target = jnp.where(slots >= 0, ((ids - owner * EXPS) * 2 + owner) * CAP + slots, -1)
    routes = jnp.pad(target.T.astype(F32), ((0, 0), (0, COLS - TOK)))
    stream_turned = lax.ppermute(jnp.concatenate([stream[0], routes], axis=0), turned, turn)
    got, stream_turned = lax.optimization_barrier((got, stream_turned))

    partial = call(
        project_kernel, shape_of(EXPS * TOK, COLS), [], [got.reshape(EXPS * TOK, COLS), out_proj]
    )
    parts = exchange(partial.reshape(HEADS, TOK, COLS), HEAD)
    resid_turned, picked = call(
        residual_kernel,
        (shape_of(TOK, COLS, dtype=F32), shape_of(ROWS, COLS)),
        [],
        [parts, stream_turned],
    )
    resid = lax.ppermute(resid_turned, turned, turn)
    weights = []
    for weight in (w_gate[0], w_up[0], w_down[0]):
        weights += [weight, lax.ppermute(weight, "tok", [(0, 1), (1, 0)])]
    rows = exchange(picked.reshape(EXPS, 2 * CAP, COLS), "exp")
    normed = call(
        norm_kernel,
        shape_of(LINE, 2 * CAP, WIDTH),
        [],
        [rows, norm_gain.reshape(1, WIDTH)],
    )
    line = exchange_lines(normed, first_lines)
    forward = call(
        forward_kernel,
        shape_of(LINE, 2 * GROUP, WIDTH),
        [core],
        [line.reshape(2 * GROUP, WIDTH), forward_order()],
    )
    arrived = exchange_lines(forward, second_lines)
    arrived, resid = lax.optimization_barrier((arrived, resid))
    produced = pl.pallas_call(
        expert_kernel,
        out_shape=shape_of(LINE, 2 * LINE, LINE * GROUP, COLS),
        in_specs=[SMEM] + [HBM] * 7,
        out_specs=HBM,
        scratch_shapes=[
            pltpu.VMEM((2, LINE * GROUP, WIDTH), BF16),
            pltpu.VMEM((6, UNITS, WIDTH), BF16),
            pltpu.VMEM((LINE, 2 * LINE, LINE * GROUP, COLS), BF16),
            pltpu.SemaphoreType.DMA((6 + 3 * LINE,)),
        ],
        compiler_params=pltpu.CompilerParams(vmem_limit_bytes=59 << 20),
    )(core, arrived, *weights)
    summed = call(
        add_kernel,
        shape_of(2 * LINE, LINE * GROUP, COLS),
        [],
        [exchange_lines(produced, first_lines)],
    )
    collected = call(
        collect_kernel,
        shape_of(ROWS, COLS),
        [core],
        [exchange_lines(summed.reshape(LINE, ROWS, COLS), second_lines), return_order()],
    )
    results = exchange(collected.reshape(EXPS, 2 * CAP, COLS), "exp")
    mixed = call(
        mix_kernel,
        shape_of(TOK, COLS, dtype=F32),
        [],
        [results.reshape(ROWS, COLS), target, gate_probs[0], resid],
    )
    return mixed[None]


def solution(mesh):
    split = Mesh(
        mesh.devices.reshape(mesh.shape["tok"], LINE, LINE, mesh.shape["exp"]),
        ("tok", "head_0", "head_1", "exp"),
    )
    in_specs = (
        P("exp", "tok", HEAD),
        P(HEAD, "exp"),
        P("exp", "tok", HEAD),
        P(),
        P("exp", "tok", None),
        P("exp", "tok", None),
        P("exp", "tok", None),
        P(("tok", "exp"), HEAD, None),
        P(("tok", "exp"), HEAD, None),
        P(("tok", "exp"), HEAD, None),
    )
    return jax.shard_map(
        on_device,
        mesh=split,
        in_specs=in_specs,
        out_specs=P("exp", "tok", HEAD),
        check_vma=False,
    )
```

```python
import jax
import jax.numpy as jnp
import numpy as np
from jax import lax
from jax.experimental import pallas as pl
from jax.experimental.pallas import tpu as pltpu
from jax.sharding import Mesh
from jax.sharding import PartitionSpec as P

CAP = 12
LINE = 4
UNITS = 192
GROUP = LINE * CAP
TOK = 32
COLS = 256
HEADS = 16
EXPS = 16
WIDTH = HEADS * COLS
ROWS = 2 * EXPS * CAP
HEAD = ("head_0", "head_1")
PLANE = ("tok", "head_0", "head_1")
EPS = 1e-05
BF16 = jnp.bfloat16
F32 = jnp.float32

VMEM = pl.BlockSpec(memory_space=pltpu.VMEM)
HBM = pl.BlockSpec(memory_space=pltpu.HBM)
SMEM = pl.BlockSpec(memory_space=pltpu.SMEM)


def call(kernel, out_shape, scalars, arrays, mib=12):
    return pl.pallas_call(
        kernel,
        out_shape=out_shape,
        in_specs=[SMEM] * len(scalars) + [VMEM] * len(arrays),
        out_specs=jax.tree.map(lambda _: VMEM, out_shape),
        compiler_params=pltpu.CompilerParams(vmem_limit_bytes=mib << 20),
    )(*scalars, *arrays)


def shape_of(*dims, dtype=BF16):
    return jax.ShapeDtypeStruct(dims, dtype)


def exchange(x, axes):
    return lax.all_to_all(x, axes, split_axis=0, concat_axis=0, tiled=True)


def project_kernel(rows_ref, weight_ref, partial_ref):
    partial_ref[...] = jnp.dot(
        rows_ref[...], weight_ref[...], preferred_element_type=F32
    ).astype(BF16)


def residual_kernel(parts_ref, turned_ref, resid_ref, slots_ref):
    total = parts_ref[0].astype(F32)
    for index in range(1, HEADS):
        total = total + parts_ref[index].astype(F32)
    total = total + turned_ref[0:TOK, :]
    resid_ref[...] = total
    place = lax.broadcasted_iota(jnp.int32, (ROWS, TOK), 0).astype(F32)
    select = jnp.zeros((ROWS, TOK), F32)
    for choice in range(8):
        wanted = turned_ref[TOK + choice : TOK + choice + 1, 0:TOK]
        select = jnp.where(place == wanted, 1.0, select)
    picked = jnp.dot(select.astype(BF16), total.astype(BF16), preferred_element_type=F32)
    slots_ref[...] = picked.astype(BF16)


def norm_kernel(rows_ref, gain_ref, out_ref):
    squares = jnp.zeros((2 * CAP, COLS), F32)
    for block in range(EXPS):
        value = rows_ref[block].astype(F32)
        squares = squares + value * value
    scale = lax.rsqrt(jnp.sum(squares, axis=1, keepdims=True) / WIDTH + EPS)
    for block in range(EXPS):
        at = slice(block * COLS, (block + 1) * COLS)
        value = (rows_ref[block].astype(F32) * scale * gain_ref[0:1, at]).astype(BF16)
        for peer in range(LINE):
            out_ref[peer, :, at] = value


def forward_kernel(core_ref, rows_ref, order_ref, out_ref, held, sems):
    order = order_ref[core_ref[0]]
    writes = []
    for part in range(LINE):
        for block in range(part * LINE, (part + 1) * LINE):
            at = slice(block * COLS, (block + 1) * COLS)
            value = jnp.dot(order, rows_ref[:, at], preferred_element_type=F32)
            held[:, at] = value.astype(BF16)
        at = pl.ds(part * LINE * COLS, LINE * COLS)
        for peer in range(LINE):
            sem = sems.at[part * LINE + peer]
            writes.append(pltpu.make_async_copy(held.at[:, at], out_ref.at[peer, :, at], sem))
            writes[-1].start()
    for write in writes:
        write.wait()


def expert_kernel(core_ref, rows_ref, *refs):
    sources, out_ref, rows_held, both, downs, staged, sems = refs[:6], *refs[6:]
    started = []

    def start(source, target):
        copy = pltpu.make_async_copy(source, target, sems.at[len(started)])
        copy.start()
        started.append(copy)
        return copy

    inputs = []
    for number in range(2):
        copies = []
        for source in range(LINE):
            at = pl.ds(number * GROUP, GROUP)
            to = pl.ds(source * GROUP, GROUP)
            copies.append(start(rows_ref.at[source, at], rows_held.at[number, to]))
        copies.append(start(sources[number], both.at[number, pl.ds(0, UNITS)]))
        copies.append(start(sources[2 + number], both.at[number, pl.ds(UNITS, UNITS)]))
        inputs.append(copies)
    lasts = [start(sources[4 + number], downs.at[number]) for number in range(2)]
    contract = (((1,), (1,)), ((), ()))
    hidden = []
    for number in range(2):
        for copy in inputs[number]:
            copy.wait()
        product = lax.dot_general(
            rows_held[number], both[number], contract, preferred_element_type=F32
        ).T
        gate, up = product[:UNITS], product[UNITS:]
        hidden.append((gate / (1.0 + jnp.exp(-gate)) * up).astype(BF16).T)
    for copy in lasts:
        copy.wait()
    first = core_ref[0] == 0
    writes = []
    for peer in range(LINE):
        for sub in range(LINE):
            block = jnp.where(first, sub * LINE + peer, peer * LINE + sub)
            at = pl.ds(pl.multiple_of(block * COLS, COLS), COLS)
            for number in range(2):
                value = jnp.dot(hidden[number], downs[number, :, at], preferred_element_type=F32)
                staged[peer, sub * 2 + number] = value.astype(BF16)
        writes.append(start(staged.at[peer], out_ref.at[peer]))
    for write in writes:
        write.wait()


def add_kernel(parts_ref, out_ref):
    for index in range(2 * LINE):
        total = parts_ref[0, index].astype(F32)
        for source in range(1, LINE):
            total = total + parts_ref[source, index].astype(F32)
        out_ref[index] = total.astype(BF16)


def collect_kernel(core_ref, parts_ref, order_ref, out_ref):
    total = parts_ref[0].astype(F32)
    for source in range(1, LINE):
        total = total + parts_ref[source].astype(F32)
    order = order_ref[core_ref[0]]
    out_ref[...] = jnp.dot(order, total.astype(BF16), preferred_element_type=F32).astype(BF16)


def mix_kernel(results_ref, target_ref, probs_ref, resid_ref, out_ref):
    place = lax.broadcasted_iota(jnp.int32, (TOK, ROWS), 1)
    weights = jnp.zeros((TOK, ROWS), F32)
    for choice in range(8):
        hit = place == target_ref[:, choice : choice + 1]
        weights = weights + jnp.where(hit, probs_ref[:, choice : choice + 1], 0.0)
    coarse = weights.astype(BF16)
    fine = (weights - coarse.astype(F32)).astype(BF16)
    results = results_ref[...]
    mixed = jnp.dot(coarse, results, preferred_element_type=F32)
    mixed = mixed + jnp.dot(fine, results, preferred_element_type=F32)
    out_ref[...] = resid_ref[...] + mixed


def forward_order():
    order = np.zeros((2, 2 * GROUP, 2 * GROUP), np.float32)
    for core in range(2):
        for number in range(2):
            for inner in range(LINE):
                for slot in range(CAP):
                    source = (inner * 2 + (core ^ number)) * CAP + slot
                    order[core, (number * LINE + inner) * CAP + slot, source] = 1
    return jnp.asarray(order, BF16)


def return_order():
    order = np.zeros((2, ROWS, ROWS), np.float32)
    for core in range(2):
        for number in range(2):
            for outer in range(LINE):
                for inner in range(LINE):
                    image = outer * LINE + inner if core == 0 else inner * LINE + outer
                    for slot in range(CAP):
                        source = ((number * LINE + outer) * LINE + inner) * CAP + slot
                        order[core, (image * 2 + (core ^ number)) * CAP + slot, source] = 1
    return jnp.asarray(order, BF16)


def plane_lines():
    lines_x = [[[(t * LINE + y) * LINE + x for x in range(LINE)] for y in range(LINE)] for t in (0, 1)]
    lines_y = [[[(t * LINE + y) * LINE + x for y in range(LINE)] for x in range(LINE)] for t in (0, 1)]
    return lines_x[0] + lines_y[1], lines_y[0] + lines_x[1]


def exchange_lines(x, lines):
    return lax.all_to_all(
        x, PLANE, split_axis=0, concat_axis=0, tiled=True, axis_index_groups=lines
    )


def on_device(
    context, out_proj, stream, norm_gain, expert_ids, slot_ids, gate_probs, w_gate, w_up, w_down
):
    core = lax.axis_index("tok").astype(jnp.int32)[None]
    turn = [(a * EXPS + b, b * EXPS + a) for a in range(HEADS) for b in range(EXPS)]
    turned = HEAD + ("exp",)
    first_lines, second_lines = plane_lines()

    got = exchange(jnp.broadcast_to(context[0], (EXPS, TOK, COLS)), "exp")

    ids, slots = expert_ids[0], slot_ids[0]
    owner = ids // EXPS
    target = jnp.where(slots >= 0, ((ids - owner * EXPS) * 2 + owner) * CAP + slots, -1)
    routes = jnp.pad(target.T.astype(F32), ((0, 0), (0, COLS - TOK)))
    stream_turned = lax.ppermute(jnp.concatenate([stream[0], routes], axis=0), turned, turn)
    got, stream_turned = lax.optimization_barrier((got, stream_turned))

    weights = []
    for weight in (w_gate[0], w_up[0], w_down[0]):
        weights += [weight, lax.ppermute(weight, "tok", [(0, 1), (1, 0)])]
    partial = call(
        project_kernel, shape_of(EXPS * TOK, COLS), [], [got.reshape(EXPS * TOK, COLS), out_proj]
    )
    parts = exchange(partial.reshape(HEADS, TOK, COLS), HEAD)
    resid_turned, picked = call(
        residual_kernel,
        (shape_of(TOK, COLS, dtype=F32), shape_of(ROWS, COLS)),
        [],
        [parts, stream_turned],
    )
    resid = lax.ppermute(resid_turned, turned, turn)
    rows = exchange(picked.reshape(EXPS, 2 * CAP, COLS), "exp")
    normed = call(
        norm_kernel,
        shape_of(LINE, 2 * CAP, WIDTH),
        [],
        [rows, norm_gain.reshape(1, WIDTH)],
    )
    line = exchange_lines(normed, first_lines)
    line, *weights[1::2] = lax.optimization_barrier((line, *weights[1::2]))
    forward = pl.pallas_call(
        forward_kernel,
        out_shape=shape_of(LINE, 2 * GROUP, WIDTH),
        in_specs=[SMEM, VMEM, VMEM],
        out_specs=HBM,
        scratch_shapes=[
            pltpu.VMEM((2 * GROUP, WIDTH), BF16),
            pltpu.SemaphoreType.DMA((LINE * LINE,)),
        ],
        compiler_params=pltpu.CompilerParams(vmem_limit_bytes=12 << 20),
    )(core, line.reshape(2 * GROUP, WIDTH), forward_order())
    arrived = exchange_lines(forward, second_lines)
    arrived, resid = lax.optimization_barrier((arrived, resid))
    produced = pl.pallas_call(
        expert_kernel,
        out_shape=shape_of(LINE, 2 * LINE, LINE * GROUP, COLS),
        in_specs=[SMEM] + [HBM] * 7,
        out_specs=HBM,
        scratch_shapes=[
            pltpu.VMEM((2, LINE * GROUP, WIDTH), BF16),
            pltpu.VMEM((2, 2 * UNITS, WIDTH), BF16),
            pltpu.VMEM((2, UNITS, WIDTH), BF16),
            pltpu.VMEM((LINE, 2 * LINE, LINE * GROUP, COLS), BF16),
            pltpu.SemaphoreType.DMA((6 + 3 * LINE,)),
        ],
        compiler_params=pltpu.CompilerParams(vmem_limit_bytes=59 << 20),
    )(core, arrived, *weights)
    summed = call(
        add_kernel,
        shape_of(2 * LINE, LINE * GROUP, COLS),
        [],
        [exchange_lines(produced, first_lines)],
    )
    collected = call(
        collect_kernel,
        shape_of(ROWS, COLS),
        [core],
        [exchange_lines(summed.reshape(LINE, ROWS, COLS), second_lines), return_order()],
    )
    results = exchange(collected.reshape(EXPS, 2 * CAP, COLS), "exp")
    mixed = call(
        mix_kernel,
        shape_of(TOK, COLS, dtype=F32),
        [],
        [results.reshape(ROWS, COLS), target, gate_probs[0], resid],
    )
    return mixed[None]


def solution(mesh):
    split = Mesh(
        mesh.devices.reshape(mesh.shape["tok"], LINE, LINE, mesh.shape["exp"]),
        ("tok", "head_0", "head_1", "exp"),
    )
    in_specs = (
        P("exp", "tok", HEAD),
        P(HEAD, "exp"),
        P("exp", "tok", HEAD),
        P(),
        P("exp", "tok", None),
        P("exp", "tok", None),
        P("exp", "tok", None),
        P(("tok", "exp"), HEAD, None),
        P(("tok", "exp"), HEAD, None),
        P(("tok", "exp"), HEAD, None),
    )
    return jax.shard_map(
        on_device,
        mesh=split,
        in_specs=in_specs,
        out_specs=P("exp", "tok", HEAD),
        check_vma=False,
    )
```

```python
import jax
import jax.numpy as jnp
import numpy as np
from jax import lax
from jax.experimental import pallas as pl
from jax.experimental.pallas import tpu as pltpu
from jax.sharding import Mesh
from jax.sharding import PartitionSpec as P

CAP = 12
LINE = 4
UNITS = 192
GROUP = LINE * CAP
TOK = 32
COLS = 256
HEADS = 16
EXPS = 16
WIDTH = HEADS * COLS
ROWS = 2 * EXPS * CAP
HEAD = ("head_0", "head_1")
PLANE = ("tok", "head_0", "head_1")
EPS = 1e-05
BF16 = jnp.bfloat16
F32 = jnp.float32

VMEM = pl.BlockSpec(memory_space=pltpu.VMEM)
HBM = pl.BlockSpec(memory_space=pltpu.HBM)
SMEM = pl.BlockSpec(memory_space=pltpu.SMEM)


def call(kernel, out_shape, scalars, arrays, mib=12):
    moved = sum(a.size * a.dtype.itemsize for a in arrays)
    return pl.pallas_call(
        kernel,
        out_shape=out_shape,
        in_specs=[SMEM] * len(scalars) + [VMEM] * len(arrays),
        out_specs=jax.tree.map(lambda _: VMEM, out_shape),
        compiler_params=pltpu.CompilerParams(vmem_limit_bytes=mib << 20),
        cost_estimate=pl.CostEstimate(flops=1 << 24, bytes_accessed=2 * moved, transcendentals=0),
    )(*scalars, *arrays)


def shape_of(*dims, dtype=BF16):
    return jax.ShapeDtypeStruct(dims, dtype)


def exchange(x, axes):
    return lax.all_to_all(x, axes, split_axis=0, concat_axis=0, tiled=True)


def project_kernel(rows_ref, weight_ref, partial_ref):
    partial_ref[...] = jnp.dot(
        rows_ref[...], weight_ref[...], preferred_element_type=F32
    ).astype(BF16)


def residual_kernel(parts_ref, turned_ref, resid_ref, slots_ref):
    total = parts_ref[0].astype(F32)
    for index in range(1, HEADS):
        total = total + parts_ref[index].astype(F32)
    total = total + turned_ref[0:TOK, :]
    resid_ref[...] = total
    place = lax.broadcasted_iota(jnp.int32, (ROWS, TOK), 0).astype(F32)
    select = jnp.zeros((ROWS, TOK), F32)
    for choice in range(8):
        wanted = turned_ref[TOK + choice : TOK + choice + 1, 0:TOK]
        select = jnp.where(place == wanted, 1.0, select)
    picked = jnp.dot(select.astype(BF16), total.astype(BF16), preferred_element_type=F32)
    slots_ref[...] = picked.astype(BF16)


def norm_kernel(rows_ref, gain_ref, out_ref):
    squares = jnp.zeros((2 * CAP, COLS), F32)
    for block in range(EXPS):
        value = rows_ref[block].astype(F32)
        squares = squares + value * value
    scale = lax.rsqrt(jnp.sum(squares, axis=1, keepdims=True) / WIDTH + EPS)
    for block in range(EXPS):
        at = slice(block * COLS, (block + 1) * COLS)
        value = (rows_ref[block].astype(F32) * scale * gain_ref[0:1, at]).astype(BF16)
        for peer in range(LINE):
            out_ref[peer, :, at] = value


def forward_kernel(core_ref, rows_ref, order_ref, out_ref, held, sems):
    order = order_ref[core_ref[0]]
    writes = []
    for part in range(LINE):
        for block in range(part * LINE, (part + 1) * LINE):
            at = slice(block * COLS, (block + 1) * COLS)
            value = jnp.dot(order, rows_ref[:, at], preferred_element_type=F32)
            held[:, at] = value.astype(BF16)
        at = pl.ds(part * LINE * COLS, LINE * COLS)
        for peer in range(LINE):
            sem = sems.at[part * LINE + peer]
            writes.append(pltpu.make_async_copy(held.at[:, at], out_ref.at[peer, :, at], sem))
            writes[-1].start()
    for write in writes:
        write.wait()


def hold_kernel(*refs):
    sources, held, sems = refs[:6], *refs[6:]
    copies = []
    for number in range(2):
        for part in range(3):
            place = held.at[pl.ds((3 * number + part) * UNITS, UNITS)]
            sem = sems.at[len(copies)]
            copies.append(pltpu.make_async_copy(sources[2 * part + number], place, sem))
            copies[-1].start()
    for copy in copies:
        copy.wait()


def expert_kernel(core_ref, rows_ref, held_ref, out_ref, held, sems):
    loads = []
    for number in range(2):
        for part, units in ((0, 2 * UNITS), (2 * UNITS, UNITS)):
            at = pl.ds(3 * number * UNITS + part, units)
            loads.append(pltpu.make_async_copy(held_ref.at[at], held.at[at], sems.at[len(loads)]))
            loads[-1].start()
    contract = (((1,), (1,)), ((), ()))
    first = core_ref[0] == 0
    for number in range(2):
        rows = rows_ref[:, number * GROUP : (number + 1) * GROUP, :].reshape(LINE * GROUP, WIDTH)
        base = 3 * number * UNITS
        loads[2 * number].wait()
        product = lax.dot_general(
            rows, held[base : base + 2 * UNITS], contract, preferred_element_type=F32
        ).T
        gate, up = product[:UNITS], product[UNITS:]
        hidden = (gate / (1.0 + jnp.exp(-gate)) * up).astype(BF16).T
        loads[2 * number + 1].wait()
        down = pl.ds(base + 2 * UNITS, UNITS)
        for peer in range(LINE):
            for sub in range(LINE):
                block = jnp.where(first, sub * LINE + peer, peer * LINE + sub)
                at = pl.ds(pl.multiple_of(block * COLS, COLS), COLS)
                value = jnp.dot(hidden, held[down, at], preferred_element_type=F32)
                out_ref[peer, sub * 2 + number] = value.astype(BF16)


def add_kernel(parts_ref, out_ref):
    for index in range(2 * LINE):
        total = parts_ref[0, index].astype(F32)
        for source in range(1, LINE):
            total = total + parts_ref[source, index].astype(F32)
        out_ref[index] = total.astype(BF16)


def collect_kernel(core_ref, parts_ref, order_ref, out_ref):
    total = parts_ref[0].astype(F32)
    for source in range(1, LINE):
        total = total + parts_ref[source].astype(F32)
    order = order_ref[core_ref[0]]
    out_ref[...] = jnp.dot(order, total.astype(BF16), preferred_element_type=F32).astype(BF16)


def mix_kernel(results_ref, target_ref, probs_ref, resid_ref, out_ref):
    place = lax.broadcasted_iota(jnp.int32, (TOK, ROWS), 1)
    weights = jnp.zeros((TOK, ROWS), F32)
    for choice in range(8):
        hit = place == target_ref[:, choice : choice + 1]
        weights = weights + jnp.where(hit, probs_ref[:, choice : choice + 1], 0.0)
    coarse = weights.astype(BF16)
    fine = (weights - coarse.astype(F32)).astype(BF16)
    results = results_ref[...]
    mixed = jnp.dot(coarse, results, preferred_element_type=F32)
    mixed = mixed + jnp.dot(fine, results, preferred_element_type=F32)
    out_ref[...] = resid_ref[...] + mixed


def forward_order():
    order = np.zeros((2, 2 * GROUP, 2 * GROUP), np.float32)
    for core in range(2):
        for number in range(2):
            for inner in range(LINE):
                for slot in range(CAP):
                    source = (inner * 2 + (core ^ number)) * CAP + slot
                    order[core, (number * LINE + inner) * CAP + slot, source] = 1
    return jnp.asarray(order, BF16)


def return_order():
    order = np.zeros((2, ROWS, ROWS), np.float32)
    for core in range(2):
        for number in range(2):
            for outer in range(LINE):
                for inner in range(LINE):
                    image = outer * LINE + inner if core == 0 else inner * LINE + outer
                    for slot in range(CAP):
                        source = ((number * LINE + outer) * LINE + inner) * CAP + slot
                        order[core, (image * 2 + (core ^ number)) * CAP + slot, source] = 1
    return jnp.asarray(order, BF16)


def plane_lines():
    lines_x = [[[(t * LINE + y) * LINE + x for x in range(LINE)] for y in range(LINE)] for t in (0, 1)]
    lines_y = [[[(t * LINE + y) * LINE + x for y in range(LINE)] for x in range(LINE)] for t in (0, 1)]
    return lines_x[0] + lines_y[1], lines_y[0] + lines_x[1]


def exchange_lines(x, lines):
    return lax.all_to_all(
        x, PLANE, split_axis=0, concat_axis=0, tiled=True, axis_index_groups=lines
    )


def on_device(
    context, out_proj, stream, norm_gain, expert_ids, slot_ids, gate_probs, w_gate, w_up, w_down
):
    core = lax.axis_index("tok").astype(jnp.int32)[None]
    turn = [(a * EXPS + b, b * EXPS + a) for a in range(HEADS) for b in range(EXPS)]
    turned = HEAD + ("exp",)
    first_lines, second_lines = plane_lines()

    got = exchange(jnp.broadcast_to(context[0], (EXPS, TOK, COLS)), "exp")

    ids, slots = expert_ids[0], slot_ids[0]
    owner = ids // EXPS
    target = jnp.where(slots >= 0, ((ids - owner * EXPS) * 2 + owner) * CAP + slots, -1)
    routes = jnp.pad(target.T.astype(F32), ((0, 0), (0, COLS - TOK)))
    stream_turned = lax.ppermute(jnp.concatenate([stream[0], routes], axis=0), turned, turn)
    got, stream_turned = lax.optimization_barrier((got, stream_turned))

    weights = []
    for weight in (w_gate[0], w_up[0], w_down[0]):
        weights += [weight, lax.ppermute(weight, "tok", [(0, 1), (1, 0)])]
    partial = call(
        project_kernel, shape_of(EXPS * TOK, COLS), [], [got.reshape(EXPS * TOK, COLS), out_proj]
    )
    parts = exchange(partial.reshape(HEADS, TOK, COLS), HEAD)
    resid_turned, picked = call(
        residual_kernel,
        (shape_of(TOK, COLS, dtype=F32), shape_of(ROWS, COLS)),
        [],
        [parts, stream_turned],
    )
    resid = lax.ppermute(resid_turned, turned, turn)
    rows = exchange(picked.reshape(EXPS, 2 * CAP, COLS), "exp")
    normed = call(
        norm_kernel,
        shape_of(LINE, 2 * CAP, WIDTH),
        [],
        [rows, norm_gain.reshape(1, WIDTH)],
    )
    line = exchange_lines(normed, first_lines)
    line, *weights[1::2] = lax.optimization_barrier((line, *weights[1::2]))
    forward = pl.pallas_call(
        forward_kernel,
        out_shape=shape_of(LINE, 2 * GROUP, WIDTH),
        in_specs=[SMEM, VMEM, VMEM],
        out_specs=HBM,
        scratch_shapes=[
            pltpu.VMEM((2 * GROUP, WIDTH), BF16),
            pltpu.SemaphoreType.DMA((LINE * LINE,)),
        ],
        compiler_params=pltpu.CompilerParams(vmem_limit_bytes=12 << 20),
    )(core, line.reshape(2 * GROUP, WIDTH), forward_order())
    arrived = exchange_lines(forward, second_lines)
    arrived, resid = lax.optimization_barrier((arrived, resid))
    held = pl.pallas_call(
        hold_kernel,
        out_shape=shape_of(6 * UNITS, WIDTH),
        in_specs=[HBM] * 6,
        out_specs=HBM,
        scratch_shapes=[pltpu.SemaphoreType.DMA((6,))],
        compiler_params=pltpu.CompilerParams(vmem_limit_bytes=60 << 20),
        cost_estimate=pl.CostEstimate(flops=0, bytes_accessed=18 << 20, transcendentals=0),
    )(*weights)
    produced = pl.pallas_call(
        expert_kernel,
        out_shape=shape_of(LINE, 2 * LINE, LINE * GROUP, COLS),
        in_specs=[SMEM, VMEM, HBM],
        out_specs=VMEM,
        scratch_shapes=[pltpu.VMEM((6 * UNITS, WIDTH), BF16), pltpu.SemaphoreType.DMA((4,))],
        compiler_params=pltpu.CompilerParams(vmem_limit_bytes=44 << 20),
        cost_estimate=pl.CostEstimate(flops=1 << 31, bytes_accessed=16 << 20, transcendentals=0),
    )(core, arrived, held)
    summed = call(
        add_kernel,
        shape_of(2 * LINE, LINE * GROUP, COLS),
        [],
        [exchange_lines(produced, first_lines)],
    )
    collected = call(
        collect_kernel,
        shape_of(ROWS, COLS),
        [core],
        [exchange_lines(summed.reshape(LINE, ROWS, COLS), second_lines), return_order()],
    )
    results = exchange(collected.reshape(EXPS, 2 * CAP, COLS), "exp")
    mixed = call(
        mix_kernel,
        shape_of(TOK, COLS, dtype=F32),
        [],
        [results.reshape(ROWS, COLS), target, gate_probs[0], resid],
    )
    return mixed[None]


def solution(mesh):
    split = Mesh(
        mesh.devices.reshape(mesh.shape["tok"], LINE, LINE, mesh.shape["exp"]),
        ("tok", "head_0", "head_1", "exp"),
    )
    in_specs = (
        P("exp", "tok", HEAD),
        P(HEAD, "exp"),
        P("exp", "tok", HEAD),
        P(),
        P("exp", "tok", None),
        P("exp", "tok", None),
        P("exp", "tok", None),
        P(("tok", "exp"), HEAD, None),
        P(("tok", "exp"), HEAD, None),
        P(("tok", "exp"), HEAD, None),
    )
    return jax.shard_map(
        on_device,
        mesh=split,
        in_specs=in_specs,
        out_specs=P("exp", "tok", HEAD),
        check_vma=False,
    )
```

```python
import jax
import jax.numpy as jnp
import numpy as np
from jax import lax
from jax.experimental import pallas as pl
from jax.experimental.pallas import tpu as pltpu
from jax.sharding import Mesh
from jax.sharding import PartitionSpec as P

CAP = 12
LINE = 4
UNITS = 192
GROUP = LINE * CAP
TOK = 32
COLS = 256
HEADS = 16
EXPS = 16
WIDTH = HEADS * COLS
ROWS = 2 * EXPS * CAP
HEAD = ("head_0", "head_1")
PLANE = ("tok", "head_0", "head_1")
EPS = 1e-05
BF16 = jnp.bfloat16
F32 = jnp.float32

VMEM = pl.BlockSpec(memory_space=pltpu.VMEM)
HBM = pl.BlockSpec(memory_space=pltpu.HBM)
SMEM = pl.BlockSpec(memory_space=pltpu.SMEM)


def call(kernel, out_shape, scalars, arrays, mib=12):
    moved = sum(a.size * a.dtype.itemsize for a in arrays)
    return pl.pallas_call(
        kernel,
        out_shape=out_shape,
        in_specs=[SMEM] * len(scalars) + [VMEM] * len(arrays),
        out_specs=jax.tree.map(lambda _: VMEM, out_shape),
        compiler_params=pltpu.CompilerParams(vmem_limit_bytes=mib << 20),
        cost_estimate=pl.CostEstimate(flops=1 << 24, bytes_accessed=2 * moved, transcendentals=0),
    )(*scalars, *arrays)


def shape_of(*dims, dtype=BF16):
    return jax.ShapeDtypeStruct(dims, dtype)


def exchange(x, axes):
    return lax.all_to_all(x, axes, split_axis=0, concat_axis=0, tiled=True)


def project_kernel(rows_ref, weight_ref, partial_ref):
    partial_ref[...] = jnp.dot(
        rows_ref[...], weight_ref[...], preferred_element_type=F32
    ).astype(BF16)


def residual_kernel(parts_ref, turned_ref, resid_ref, slots_ref):
    total = parts_ref[0].astype(F32)
    for index in range(1, HEADS):
        total = total + parts_ref[index].astype(F32)
    total = total + turned_ref[0:TOK, :]
    resid_ref[...] = total
    place = lax.broadcasted_iota(jnp.int32, (ROWS, TOK), 0).astype(F32)
    select = jnp.zeros((ROWS, TOK), F32)
    for choice in range(8):
        wanted = turned_ref[TOK + choice : TOK + choice + 1, 0:TOK]
        select = jnp.where(place == wanted, 1.0, select)
    picked = jnp.dot(select.astype(BF16), total.astype(BF16), preferred_element_type=F32)
    slots_ref[...] = picked.astype(BF16)


def norm_kernel(rows_ref, gain_ref, out_ref):
    squares = jnp.zeros((2 * CAP, COLS), F32)
    for block in range(EXPS):
        value = rows_ref[block].astype(F32)
        squares = squares + value * value
    scale = lax.rsqrt(jnp.sum(squares, axis=1, keepdims=True) / WIDTH + EPS)
    for block in range(EXPS):
        at = slice(block * COLS, (block + 1) * COLS)
        value = (rows_ref[block].astype(F32) * scale * gain_ref[0:1, at]).astype(BF16)
        for peer in range(LINE):
            out_ref[peer, :, at] = value


def forward_kernel(core_ref, rows_ref, order_ref, out_ref, held, sems):
    order = order_ref[core_ref[0]]
    writes = []
    for part in range(LINE):
        for block in range(part * LINE, (part + 1) * LINE):
            at = slice(block * COLS, (block + 1) * COLS)
            value = jnp.dot(order, rows_ref[:, at], preferred_element_type=F32)
            held[:, at] = value.astype(BF16)
        at = pl.ds(part * LINE * COLS, LINE * COLS)
        for peer in range(LINE):
            sem = sems.at[part * LINE + peer]
            writes.append(pltpu.make_async_copy(held.at[:, at], out_ref.at[peer, :, at], sem))
            writes[-1].start()
    for write in writes:
        write.wait()


def stack_kernel(*refs):
    sources, out_ref, held, sems = refs[:3], *refs[3:]
    loads, writes = [], []
    for part in range(3):
        loads.append(pltpu.make_async_copy(sources[part], held.at[part], sems.at[part]))
        at = pl.ds(part * UNITS, UNITS)
        writes.append(pltpu.make_async_copy(held.at[part], out_ref.at[at], sems.at[3 + part]))
    for load in loads:
        load.start()
    for load, write in zip(loads, writes):
        load.wait()
        write.start()
    for write in writes:
        write.wait()


def expert_kernel(core_ref, rows_ref, own_ref, other_ref, out_ref, held, sems):
    loads = []
    for number, source in enumerate((own_ref, other_ref)):
        for part, units in ((0, 2 * UNITS), (2 * UNITS, UNITS)):
            at = pl.ds(3 * number * UNITS + part, units)
            sem = sems.at[len(loads)]
            loads.append(pltpu.make_async_copy(source.at[pl.ds(part, units)], held.at[at], sem))
            loads[-1].start()
    contract = (((1,), (1,)), ((), ()))
    first = core_ref[0] == 0
    for number in range(2):
        rows = rows_ref[:, number * GROUP : (number + 1) * GROUP, :].reshape(LINE * GROUP, WIDTH)
        base = 3 * number * UNITS
        loads[2 * number].wait()
        product = lax.dot_general(
            rows, held[base : base + 2 * UNITS], contract, preferred_element_type=F32
        ).T
        gate, up = product[:UNITS], product[UNITS:]
        hidden = (gate / (1.0 + jnp.exp(-gate)) * up).astype(BF16).T
        loads[2 * number + 1].wait()
        down = pl.ds(base + 2 * UNITS, UNITS)
        for peer in range(LINE):
            for sub in range(LINE):
                block = jnp.where(first, sub * LINE + peer, peer * LINE + sub)
                at = pl.ds(pl.multiple_of(block * COLS, COLS), COLS)
                value = jnp.dot(hidden, held[down, at], preferred_element_type=F32)
                out_ref[peer, sub * 2 + number] = value.astype(BF16)


def add_kernel(parts_ref, out_ref):
    for index in range(2 * LINE):
        total = parts_ref[0, index].astype(F32)
        for source in range(1, LINE):
            total = total + parts_ref[source, index].astype(F32)
        out_ref[index] = total.astype(BF16)


def collect_kernel(core_ref, parts_ref, order_ref, out_ref):
    total = parts_ref[0].astype(F32)
    for source in range(1, LINE):
        total = total + parts_ref[source].astype(F32)
    order = order_ref[core_ref[0]]
    out_ref[...] = jnp.dot(order, total.astype(BF16), preferred_element_type=F32).astype(BF16)


def mix_kernel(results_ref, target_ref, probs_ref, resid_ref, out_ref):
    place = lax.broadcasted_iota(jnp.int32, (TOK, ROWS), 1)
    weights = jnp.zeros((TOK, ROWS), F32)
    for choice in range(8):
        hit = place == target_ref[:, choice : choice + 1]
        weights = weights + jnp.where(hit, probs_ref[:, choice : choice + 1], 0.0)
    coarse = weights.astype(BF16)
    fine = (weights - coarse.astype(F32)).astype(BF16)
    results = results_ref[...]
    mixed = jnp.dot(coarse, results, preferred_element_type=F32)
    mixed = mixed + jnp.dot(fine, results, preferred_element_type=F32)
    out_ref[...] = resid_ref[...] + mixed


def forward_order():
    order = np.zeros((2, 2 * GROUP, 2 * GROUP), np.float32)
    for core in range(2):
        for number in range(2):
            for inner in range(LINE):
                for slot in range(CAP):
                    source = (inner * 2 + (core ^ number)) * CAP + slot
                    order[core, (number * LINE + inner) * CAP + slot, source] = 1
    return jnp.asarray(order, BF16)


def return_order():
    order = np.zeros((2, ROWS, ROWS), np.float32)
    for core in range(2):
        for number in range(2):
            for outer in range(LINE):
                for inner in range(LINE):
                    image = outer * LINE + inner if core == 0 else inner * LINE + outer
                    for slot in range(CAP):
                        source = ((number * LINE + outer) * LINE + inner) * CAP + slot
                        order[core, (image * 2 + (core ^ number)) * CAP + slot, source] = 1
    return jnp.asarray(order, BF16)


def plane_lines():
    lines_x = [[[(t * LINE + y) * LINE + x for x in range(LINE)] for y in range(LINE)] for t in (0, 1)]
    lines_y = [[[(t * LINE + y) * LINE + x for y in range(LINE)] for x in range(LINE)] for t in (0, 1)]
    return lines_x[0] + lines_y[1], lines_y[0] + lines_x[1]


def exchange_lines(x, lines):
    return lax.all_to_all(
        x, PLANE, split_axis=0, concat_axis=0, tiled=True, axis_index_groups=lines
    )


def on_device(
    context, out_proj, stream, norm_gain, expert_ids, slot_ids, gate_probs, w_gate, w_up, w_down
):
    core = lax.axis_index("tok").astype(jnp.int32)[None]
    turn = [(a * EXPS + b, b * EXPS + a) for a in range(HEADS) for b in range(EXPS)]
    turned = HEAD + ("exp",)
    first_lines, second_lines = plane_lines()

    got = exchange(jnp.broadcast_to(context[0], (EXPS, TOK, COLS)), "exp")

    ids, slots = expert_ids[0], slot_ids[0]
    owner = ids // EXPS
    target = jnp.where(slots >= 0, ((ids - owner * EXPS) * 2 + owner) * CAP + slots, -1)
    routes = jnp.pad(target.T.astype(F32), ((0, 0), (0, COLS - TOK)))
    stream_turned = lax.ppermute(jnp.concatenate([stream[0], routes], axis=0), turned, turn)
    own = pl.pallas_call(
        stack_kernel,
        out_shape=shape_of(3 * UNITS, WIDTH),
        in_specs=[HBM] * 3,
        out_specs=HBM,
        scratch_shapes=[pltpu.VMEM((3, UNITS, WIDTH), BF16), pltpu.SemaphoreType.DMA((6,))],
        compiler_params=pltpu.CompilerParams(vmem_limit_bytes=60 << 20),
        cost_estimate=pl.CostEstimate(flops=0, bytes_accessed=9 << 20, transcendentals=0),
    )(w_gate[0], w_up[0], w_down[0])
    got, stream_turned, own = lax.optimization_barrier((got, stream_turned, own))

    other = lax.ppermute(own, "tok", [(0, 1), (1, 0)])
    partial = call(
        project_kernel, shape_of(EXPS * TOK, COLS), [], [got.reshape(EXPS * TOK, COLS), out_proj]
    )
    parts = exchange(partial.reshape(HEADS, TOK, COLS), HEAD)
    resid_turned, picked = call(
        residual_kernel,
        (shape_of(TOK, COLS, dtype=F32), shape_of(ROWS, COLS)),
        [],
        [parts, stream_turned],
    )
    resid = lax.ppermute(resid_turned, turned, turn)
    rows = exchange(picked.reshape(EXPS, 2 * CAP, COLS), "exp")
    normed = call(
        norm_kernel,
        shape_of(LINE, 2 * CAP, WIDTH),
        [],
        [rows, norm_gain.reshape(1, WIDTH)],
    )
    line = exchange_lines(normed, first_lines)
    line, other = lax.optimization_barrier((line, other))
    forward = pl.pallas_call(
        forward_kernel,
        out_shape=shape_of(LINE, 2 * GROUP, WIDTH),
        in_specs=[SMEM, VMEM, VMEM],
        out_specs=HBM,
        scratch_shapes=[
            pltpu.VMEM((2 * GROUP, WIDTH), BF16),
            pltpu.SemaphoreType.DMA((LINE * LINE,)),
        ],
        compiler_params=pltpu.CompilerParams(vmem_limit_bytes=12 << 20),
    )(core, line.reshape(2 * GROUP, WIDTH), forward_order())
    arrived = exchange_lines(forward, second_lines)
    arrived, resid = lax.optimization_barrier((arrived, resid))
    produced = pl.pallas_call(
        expert_kernel,
        out_shape=shape_of(LINE, 2 * LINE, LINE * GROUP, COLS),
        in_specs=[SMEM, VMEM, HBM, HBM],
        out_specs=VMEM,
        scratch_shapes=[pltpu.VMEM((6 * UNITS, WIDTH), BF16), pltpu.SemaphoreType.DMA((4,))],
        compiler_params=pltpu.CompilerParams(vmem_limit_bytes=44 << 20),
        cost_estimate=pl.CostEstimate(flops=1 << 31, bytes_accessed=16 << 20, transcendentals=0),
    )(core, arrived, own, other)
    summed = call(
        add_kernel,
        shape_of(2 * LINE, LINE * GROUP, COLS),
        [],
        [exchange_lines(produced, first_lines)],
    )
    collected = call(
        collect_kernel,
        shape_of(ROWS, COLS),
        [core],
        [exchange_lines(summed.reshape(LINE, ROWS, COLS), second_lines), return_order()],
    )
    results = exchange(collected.reshape(EXPS, 2 * CAP, COLS), "exp")
    mixed = call(
        mix_kernel,
        shape_of(TOK, COLS, dtype=F32),
        [],
        [results.reshape(ROWS, COLS), target, gate_probs[0], resid],
    )
    return mixed[None]


def solution(mesh):
    split = Mesh(
        mesh.devices.reshape(mesh.shape["tok"], LINE, LINE, mesh.shape["exp"]),
        ("tok", "head_0", "head_1", "exp"),
    )
    in_specs = (
        P("exp", "tok", HEAD),
        P(HEAD, "exp"),
        P("exp", "tok", HEAD),
        P(),
        P("exp", "tok", None),
        P("exp", "tok", None),
        P("exp", "tok", None),
        P(("tok", "exp"), HEAD, None),
        P(("tok", "exp"), HEAD, None),
        P(("tok", "exp"), HEAD, None),
    )
    return jax.shard_map(
        on_device,
        mesh=split,
        in_specs=in_specs,
        out_specs=P("exp", "tok", HEAD),
        check_vma=False,
    )
```

```python
import jax
import jax.numpy as jnp
import numpy as np
from jax import lax
from jax.experimental import pallas as pl
from jax.experimental.pallas import tpu as pltpu
from jax.sharding import Mesh
from jax.sharding import PartitionSpec as P

CAP = 12
LINE = 4
UNITS = 192
GROUP = LINE * CAP
TOK = 32
COLS = 256
HEADS = 16
EXPS = 16
WIDTH = HEADS * COLS
HALF = WIDTH // 2
ROWS = 2 * EXPS * CAP
HEAD = ("head_0", "head_1")
PLANE = ("tok", "head_0", "head_1")
EPS = 1e-05
BF16 = jnp.bfloat16
F32 = jnp.float32

VMEM = pl.BlockSpec(memory_space=pltpu.VMEM)
HBM = pl.BlockSpec(memory_space=pltpu.HBM)
SMEM = pl.BlockSpec(memory_space=pltpu.SMEM)


def call(kernel, out_shape, scalars, arrays, mib=12):
    moved = sum(a.size * a.dtype.itemsize for a in arrays)
    return pl.pallas_call(
        kernel,
        out_shape=out_shape,
        in_specs=[SMEM] * len(scalars) + [VMEM] * len(arrays),
        out_specs=jax.tree.map(lambda _: VMEM, out_shape),
        compiler_params=pltpu.CompilerParams(vmem_limit_bytes=mib << 20),
        cost_estimate=pl.CostEstimate(flops=1 << 24, bytes_accessed=2 * moved, transcendentals=0),
    )(*scalars, *arrays)


def shape_of(*dims, dtype=BF16):
    return jax.ShapeDtypeStruct(dims, dtype)


def exchange(x, axes):
    return lax.all_to_all(x, axes, split_axis=0, concat_axis=0, tiled=True)


def project_kernel(rows_ref, weight_ref, partial_ref):
    partial_ref[...] = jnp.dot(
        rows_ref[...], weight_ref[...], preferred_element_type=F32
    ).astype(BF16)


def residual_kernel(parts_ref, turned_ref, resid_ref, slots_ref):
    total = parts_ref[0].astype(F32)
    for index in range(1, HEADS):
        total = total + parts_ref[index].astype(F32)
    total = total + turned_ref[0:TOK, :]
    resid_ref[...] = total
    place = lax.broadcasted_iota(jnp.int32, (ROWS, TOK), 0).astype(F32)
    select = jnp.zeros((ROWS, TOK), F32)
    for choice in range(8):
        wanted = turned_ref[TOK + choice : TOK + choice + 1, 0:TOK]
        select = jnp.where(place == wanted, 1.0, select)
    picked = jnp.dot(select.astype(BF16), total.astype(BF16), preferred_element_type=F32)
    slots_ref[...] = picked.astype(BF16)


def norm_kernel(rows_ref, gain_ref, out_ref):
    squares = jnp.zeros((2 * CAP, COLS), F32)
    for block in range(EXPS):
        value = rows_ref[block].astype(F32)
        squares = squares + value * value
    scale = lax.rsqrt(jnp.sum(squares, axis=1, keepdims=True) / WIDTH + EPS)
    for block in range(EXPS):
        at = slice(block * COLS, (block + 1) * COLS)
        value = (rows_ref[block].astype(F32) * scale * gain_ref[0:1, at]).astype(BF16)
        for peer in range(LINE):
            out_ref[peer, :, at] = value


def forward_kernel(core_ref, rows_ref, order_ref, out_ref, held, sems):
    order = order_ref[core_ref[0]]
    writes = []
    for part in range(LINE):
        for block in range(part * LINE, (part + 1) * LINE):
            at = slice(block * COLS, (block + 1) * COLS)
            value = jnp.dot(order, rows_ref[:, at], preferred_element_type=F32)
            held[:, at] = value.astype(BF16)
        at = pl.ds(part * LINE * COLS, LINE * COLS)
        for peer in range(LINE):
            sem = sems.at[part * LINE + peer]
            writes.append(pltpu.make_async_copy(held.at[:, at], out_ref.at[peer, :, at], sem))
            writes[-1].start()
    for write in writes:
        write.wait()


def stack_kernel(*refs):
    sources, out_ref, held, sems = refs[:3], *refs[3:]
    loads, writes = [], []
    for part in range(3):
        loads.append(pltpu.make_async_copy(sources[part], held.at[part], sems.at[part]))
        at = pl.ds(part * UNITS, UNITS)
        writes.append(pltpu.make_async_copy(held.at[part], out_ref.at[at], sems.at[3 + part]))
    for load in loads:
        load.start()
    for load, write in zip(loads, writes):
        load.wait()
        write.start()
    for write in writes:
        write.wait()


def expert_kernel(core_ref, rows_ref, own_ref, other_ref, out_ref, both, downs, sems):
    started = []

    def start(source, target):
        copy = pltpu.make_async_copy(source, target, sems.at[len(started)])
        copy.start()
        started.append(copy)
        return copy

    halves = [pl.ds(half * HALF, HALF) for half in range(2)]
    loads = []
    for number, source in enumerate((own_ref, other_ref)):
        for at in halves:
            gate = start(source.at[pl.ds(0, UNITS), at], both.at[number, pl.ds(0, UNITS), at])
            up = start(source.at[pl.ds(UNITS, UNITS), at], both.at[number, pl.ds(COLS, UNITS), at])
            loads.append((gate, up))
        loads.append((start(source.at[pl.ds(2 * UNITS, UNITS)], downs.at[number]),))
    for number in range(2):
        both[number, UNITS:COLS, :] = jnp.zeros((COLS - UNITS, WIDTH), BF16)
    contract = (((1,), (1,)), ((), ()))
    first = core_ref[0] == 0
    for number in range(2):
        product = jnp.zeros((LINE * GROUP, COLS + UNITS), F32)
        for half, at in enumerate(halves):
            for load in loads[3 * number + half]:
                load.wait()
            rows = rows_ref[:, number * GROUP : (number + 1) * GROUP, at]
            product = product + lax.dot_general(
                rows.reshape(LINE * GROUP, HALF),
                both[number, :, at],
                contract,
                preferred_element_type=F32,
            )
        gate, up = product[:, :UNITS], product[:, COLS:]
        hidden = (gate / (1.0 + jnp.exp(-gate)) * up).astype(BF16)
        loads[3 * number + 2][0].wait()
        for peer in range(LINE):
            for sub in range(LINE):
                block = jnp.where(first, sub * LINE + peer, peer * LINE + sub)
                at = pl.ds(pl.multiple_of(block * COLS, COLS), COLS)
                value = jnp.dot(hidden, downs[number, :, at], preferred_element_type=F32)
                out_ref[peer, sub * 2 + number] = value.astype(BF16)


def add_kernel(parts_ref, out_ref):
    for index in range(2 * LINE):
        total = parts_ref[0, index].astype(F32)
        for source in range(1, LINE):
            total = total + parts_ref[source, index].astype(F32)
        out_ref[index] = total.astype(BF16)


def collect_kernel(core_ref, parts_ref, order_ref, out_ref):
    total = parts_ref[0].astype(F32)
    for source in range(1, LINE):
        total = total + parts_ref[source].astype(F32)
    order = order_ref[core_ref[0]]
    out_ref[...] = jnp.dot(order, total.astype(BF16), preferred_element_type=F32).astype(BF16)


def mix_kernel(results_ref, target_ref, probs_ref, resid_ref, out_ref):
    place = lax.broadcasted_iota(jnp.int32, (TOK, ROWS), 1)
    weights = jnp.zeros((TOK, ROWS), F32)
    for choice in range(8):
        hit = place == target_ref[:, choice : choice + 1]
        weights = weights + jnp.where(hit, probs_ref[:, choice : choice + 1], 0.0)
    coarse = weights.astype(BF16)
    fine = (weights - coarse.astype(F32)).astype(BF16)
    results = results_ref[...]
    mixed = jnp.dot(coarse, results, preferred_element_type=F32)
    mixed = mixed + jnp.dot(fine, results, preferred_element_type=F32)
    out_ref[...] = resid_ref[...] + mixed


def forward_order():
    order = np.zeros((2, 2 * GROUP, 2 * GROUP), np.float32)
    for core in range(2):
        for number in range(2):
            for inner in range(LINE):
                for slot in range(CAP):
                    source = (inner * 2 + (core ^ number)) * CAP + slot
                    order[core, (number * LINE + inner) * CAP + slot, source] = 1
    return jnp.asarray(order, BF16)


def return_order():
    order = np.zeros((2, ROWS, ROWS), np.float32)
    for core in range(2):
        for number in range(2):
            for outer in range(LINE):
                for inner in range(LINE):
                    image = outer * LINE + inner if core == 0 else inner * LINE + outer
                    for slot in range(CAP):
                        source = ((number * LINE + outer) * LINE + inner) * CAP + slot
                        order[core, (image * 2 + (core ^ number)) * CAP + slot, source] = 1
    return jnp.asarray(order, BF16)


def plane_lines():
    lines_x = [[[(t * LINE + y) * LINE + x for x in range(LINE)] for y in range(LINE)] for t in (0, 1)]
    lines_y = [[[(t * LINE + y) * LINE + x for y in range(LINE)] for x in range(LINE)] for t in (0, 1)]
    return lines_x[0] + lines_y[1], lines_y[0] + lines_x[1]


def exchange_lines(x, lines):
    return lax.all_to_all(
        x, PLANE, split_axis=0, concat_axis=0, tiled=True, axis_index_groups=lines
    )


def on_device(
    context, out_proj, stream, norm_gain, expert_ids, slot_ids, gate_probs, w_gate, w_up, w_down
):
    core = lax.axis_index("tok").astype(jnp.int32)[None]
    turn = [(a * EXPS + b, b * EXPS + a) for a in range(HEADS) for b in range(EXPS)]
    turned = HEAD + ("exp",)
    first_lines, second_lines = plane_lines()

    got = exchange(jnp.broadcast_to(context[0], (EXPS, TOK, COLS)), "exp")

    ids, slots = expert_ids[0], slot_ids[0]
    owner = ids // EXPS
    target = jnp.where(slots >= 0, ((ids - owner * EXPS) * 2 + owner) * CAP + slots, -1)
    routes = jnp.pad(target.T.astype(F32), ((0, 0), (0, COLS - TOK)))
    stream_turned = lax.ppermute(jnp.concatenate([stream[0], routes], axis=0), turned, turn)
    own = pl.pallas_call(
        stack_kernel,
        out_shape=shape_of(3 * UNITS, WIDTH),
        in_specs=[HBM] * 3,
        out_specs=HBM,
        scratch_shapes=[pltpu.VMEM((3, UNITS, WIDTH), BF16), pltpu.SemaphoreType.DMA((6,))],
        compiler_params=pltpu.CompilerParams(vmem_limit_bytes=60 << 20),
        cost_estimate=pl.CostEstimate(flops=0, bytes_accessed=9 << 20, transcendentals=0),
    )(w_gate[0], w_up[0], w_down[0])
    got, stream_turned, own = lax.optimization_barrier((got, stream_turned, own))

    other = lax.ppermute(own, "tok", [(0, 1), (1, 0)])
    partial = call(
        project_kernel, shape_of(EXPS * TOK, COLS), [], [got.reshape(EXPS * TOK, COLS), out_proj]
    )
    parts = exchange(partial.reshape(HEADS, TOK, COLS), HEAD)
    resid_turned, picked = call(
        residual_kernel,
        (shape_of(TOK, COLS, dtype=F32), shape_of(ROWS, COLS)),
        [],
        [parts, stream_turned],
    )
    resid = lax.ppermute(resid_turned, turned, turn)
    rows = exchange(picked.reshape(EXPS, 2 * CAP, COLS), "exp")
    normed = call(
        norm_kernel,
        shape_of(LINE, 2 * CAP, WIDTH),
        [],
        [rows, norm_gain.reshape(1, WIDTH)],
    )
    line = exchange_lines(normed, first_lines)
    line, other = lax.optimization_barrier((line, other))
    forward = pl.pallas_call(
        forward_kernel,
        out_shape=shape_of(LINE, 2 * GROUP, WIDTH),
        in_specs=[SMEM, VMEM, VMEM],
        out_specs=HBM,
        scratch_shapes=[
            pltpu.VMEM((2 * GROUP, WIDTH), BF16),
            pltpu.SemaphoreType.DMA((LINE * LINE,)),
        ],
        compiler_params=pltpu.CompilerParams(vmem_limit_bytes=12 << 20),
    )(core, line.reshape(2 * GROUP, WIDTH), forward_order())
    arrived = exchange_lines(forward, second_lines)
    arrived, resid = lax.optimization_barrier((arrived, resid))
    produced = pl.pallas_call(
        expert_kernel,
        out_shape=shape_of(LINE, 2 * LINE, LINE * GROUP, COLS),
        in_specs=[SMEM, VMEM, HBM, HBM],
        out_specs=VMEM,
        scratch_shapes=[
            pltpu.VMEM((2, COLS + UNITS, WIDTH), BF16),
            pltpu.VMEM((2, UNITS, WIDTH), BF16),
            pltpu.SemaphoreType.DMA((10,)),
        ],
        compiler_params=pltpu.CompilerParams(vmem_limit_bytes=44 << 20),
        cost_estimate=pl.CostEstimate(flops=1 << 31, bytes_accessed=16 << 20, transcendentals=0),
    )(core, arrived, own, other)
    summed = call(
        add_kernel,
        shape_of(2 * LINE, LINE * GROUP, COLS),
        [],
        [exchange_lines(produced, first_lines)],
    )
    collected = call(
        collect_kernel,
        shape_of(ROWS, COLS),
        [core],
        [exchange_lines(summed.reshape(LINE, ROWS, COLS), second_lines), return_order()],
    )
    results = exchange(collected.reshape(EXPS, 2 * CAP, COLS), "exp")
    mixed = call(
        mix_kernel,
        shape_of(TOK, COLS, dtype=F32),
        [],
        [results.reshape(ROWS, COLS), target, gate_probs[0], resid],
    )
    return mixed[None]


def solution(mesh):
    split = Mesh(
        mesh.devices.reshape(mesh.shape["tok"], LINE, LINE, mesh.shape["exp"]),
        ("tok", "head_0", "head_1", "exp"),
    )
    in_specs = (
        P("exp", "tok", HEAD),
        P(HEAD, "exp"),
        P("exp", "tok", HEAD),
        P(),
        P("exp", "tok", None),
        P("exp", "tok", None),
        P("exp", "tok", None),
        P(("tok", "exp"), HEAD, None),
        P(("tok", "exp"), HEAD, None),
        P(("tok", "exp"), HEAD, None),
    )
    return jax.shard_map(
        on_device,
        mesh=split,
        in_specs=in_specs,
        out_specs=P("exp", "tok", HEAD),
        check_vma=False,
    )
```

```python
import jax
import jax.numpy as jnp
import numpy as np
from jax import lax
from jax.experimental import pallas as pl
from jax.experimental.pallas import tpu as pltpu
from jax.sharding import Mesh
from jax.sharding import PartitionSpec as P

CAP = 12
LINE = 4
UNITS = 192
GROUP = LINE * CAP
TOK = 32
COLS = 256
HEADS = 16
EXPS = 16
WIDTH = HEADS * COLS
HALF = WIDTH // 2
ROWS = 2 * EXPS * CAP
HEAD = ("head_0", "head_1")
PLANE = ("tok", "head_0", "head_1")
EPS = 1e-05
BF16 = jnp.bfloat16
F32 = jnp.float32

VMEM = pl.BlockSpec(memory_space=pltpu.VMEM)
HBM = pl.BlockSpec(memory_space=pltpu.HBM)
SMEM = pl.BlockSpec(memory_space=pltpu.SMEM)


def call(kernel, out_shape, scalars, arrays, mib=12):
    moved = sum(a.size * a.dtype.itemsize for a in arrays)
    return pl.pallas_call(
        kernel,
        out_shape=out_shape,
        in_specs=[SMEM] * len(scalars) + [VMEM] * len(arrays),
        out_specs=jax.tree.map(lambda _: VMEM, out_shape),
        compiler_params=pltpu.CompilerParams(vmem_limit_bytes=mib << 20),
        cost_estimate=pl.CostEstimate(flops=1 << 24, bytes_accessed=2 * moved, transcendentals=0),
    )(*scalars, *arrays)


def shape_of(*dims, dtype=BF16):
    return jax.ShapeDtypeStruct(dims, dtype)


def exchange(x, axes):
    return lax.all_to_all(x, axes, split_axis=0, concat_axis=0, tiled=True)


def project_kernel(rows_ref, weight_ref, partial_ref):
    partial_ref[...] = jnp.dot(
        rows_ref[...], weight_ref[...], preferred_element_type=F32
    ).astype(BF16)


def residual_kernel(parts_ref, turned_ref, resid_ref, slots_ref):
    total = parts_ref[0].astype(F32)
    for index in range(1, HEADS):
        total = total + parts_ref[index].astype(F32)
    total = total + turned_ref[0:TOK, :]
    resid_ref[...] = total
    place = lax.broadcasted_iota(jnp.int32, (ROWS, TOK), 0).astype(F32)
    select = jnp.zeros((ROWS, TOK), F32)
    for choice in range(8):
        wanted = turned_ref[TOK + choice : TOK + choice + 1, 0:TOK]
        select = jnp.where(place == wanted, 1.0, select)
    picked = jnp.dot(select.astype(BF16), total.astype(BF16), preferred_element_type=F32)
    slots_ref[...] = picked.astype(BF16)


def norm_kernel(rows_ref, gain_ref, out_ref):
    squares = jnp.zeros((2 * CAP, COLS), F32)
    for block in range(EXPS):
        value = rows_ref[block].astype(F32)
        squares = squares + value * value
    scale = lax.rsqrt(jnp.sum(squares, axis=1, keepdims=True) / WIDTH + EPS)
    for block in range(EXPS):
        at = slice(block * COLS, (block + 1) * COLS)
        value = (rows_ref[block].astype(F32) * scale * gain_ref[0:1, at]).astype(BF16)
        for peer in range(LINE):
            out_ref[peer, :, at] = value


def forward_kernel(core_ref, rows_ref, order_ref, out_ref, held, sems):
    order = order_ref[core_ref[0]]
    writes = []
    for part in range(LINE):
        for block in range(part * LINE, (part + 1) * LINE):
            at = slice(block * COLS, (block + 1) * COLS)
            value = jnp.dot(order, rows_ref[:, at], preferred_element_type=F32)
            held[:, at] = value.astype(BF16)
        at = pl.ds(part * LINE * COLS, LINE * COLS)
        for peer in range(LINE):
            sem = sems.at[part * LINE + peer]
            writes.append(pltpu.make_async_copy(held.at[:, at], out_ref.at[peer, :, at], sem))
            writes[-1].start()
    for write in writes:
        write.wait()


def stack_kernel(*refs):
    sources, out_ref, held, sems = refs[:3], *refs[3:]
    loads, writes = [], []
    for part in range(3):
        loads.append(pltpu.make_async_copy(sources[part], held.at[part], sems.at[part]))
        at = pl.ds(part * UNITS, UNITS)
        writes.append(pltpu.make_async_copy(held.at[part], out_ref.at[at], sems.at[3 + part]))
    for load in loads:
        load.start()
    for load, write in zip(loads, writes):
        load.wait()
        write.start()
    for write in writes:
        write.wait()


def expert_kernel(core_ref, rows_ref, own_ref, other_ref, out_ref, both, downs, sems):
    started = []

    def start(source, target):
        copy = pltpu.make_async_copy(source, target, sems.at[len(started)])
        copy.start()
        started.append(copy)
        return copy

    halves = [pl.ds(half * HALF, HALF) for half in range(2)]
    loads = []
    for number, source in enumerate((own_ref, other_ref)):
        for at in halves:
            gate = start(source.at[pl.ds(0, UNITS), at], both.at[number, pl.ds(0, UNITS), at])
            up = start(source.at[pl.ds(UNITS, UNITS), at], both.at[number, pl.ds(COLS, UNITS), at])
            loads.append((gate, up))
        loads.append((start(source.at[pl.ds(2 * UNITS, UNITS)], downs.at[number]),))
    for number in range(2):
        both[number, UNITS:COLS, :] = jnp.zeros((COLS - UNITS, WIDTH), BF16)
    contract = (((1,), (1,)), ((), ()))
    first = core_ref[0] == 0
    for number in range(2):
        product = jnp.zeros((LINE * GROUP, COLS + UNITS), F32)
        for half, at in enumerate(halves):
            for load in loads[3 * number + half]:
                load.wait()
            rows = rows_ref[:, number * GROUP : (number + 1) * GROUP, at]
            product = product + lax.dot_general(
                rows.reshape(LINE * GROUP, HALF),
                both[number, :, at],
                contract,
                preferred_element_type=F32,
            )
        gate, up = product[:, :UNITS], product[:, COLS:]
        hidden = (gate / (1.0 + jnp.exp(-gate)) * up).astype(BF16)
        loads[3 * number + 2][0].wait()
        for block in range(HEADS):
            outer, inner = block // LINE, block % LINE
            peer = jnp.where(first, inner, outer)
            sub = jnp.where(first, outer, inner)
            value = jnp.dot(
                hidden,
                downs[number, :, block * COLS : (block + 1) * COLS],
                preferred_element_type=F32,
            )
            out_ref[peer, sub * 2 + number] = value.astype(BF16)


def add_kernel(parts_ref, out_ref):
    for index in range(2 * LINE):
        total = parts_ref[0, index].astype(F32)
        for source in range(1, LINE):
            total = total + parts_ref[source, index].astype(F32)
        out_ref[index] = total.astype(BF16)


def collect_kernel(core_ref, parts_ref, order_ref, out_ref):
    total = parts_ref[0].astype(F32)
    for source in range(1, LINE):
        total = total + parts_ref[source].astype(F32)
    order = order_ref[core_ref[0]]
    out_ref[...] = jnp.dot(order, total.astype(BF16), preferred_element_type=F32).astype(BF16)


def mix_kernel(results_ref, target_ref, probs_ref, resid_ref, out_ref):
    place = lax.broadcasted_iota(jnp.int32, (TOK, ROWS), 1)
    weights = jnp.zeros((TOK, ROWS), F32)
    for choice in range(8):
        hit = place == target_ref[:, choice : choice + 1]
        weights = weights + jnp.where(hit, probs_ref[:, choice : choice + 1], 0.0)
    coarse = weights.astype(BF16)
    fine = (weights - coarse.astype(F32)).astype(BF16)
    results = results_ref[...]
    mixed = jnp.dot(coarse, results, preferred_element_type=F32)
    mixed = mixed + jnp.dot(fine, results, preferred_element_type=F32)
    out_ref[...] = resid_ref[...] + mixed


def forward_order():
    order = np.zeros((2, 2 * GROUP, 2 * GROUP), np.float32)
    for core in range(2):
        for number in range(2):
            for inner in range(LINE):
                for slot in range(CAP):
                    source = (inner * 2 + (core ^ number)) * CAP + slot
                    order[core, (number * LINE + inner) * CAP + slot, source] = 1
    return jnp.asarray(order, BF16)


def return_order():
    order = np.zeros((2, ROWS, ROWS), np.float32)
    for core in range(2):
        for number in range(2):
            for outer in range(LINE):
                for inner in range(LINE):
                    image = outer * LINE + inner if core == 0 else inner * LINE + outer
                    for slot in range(CAP):
                        source = ((number * LINE + outer) * LINE + inner) * CAP + slot
                        order[core, (image * 2 + (core ^ number)) * CAP + slot, source] = 1
    return jnp.asarray(order, BF16)


def plane_lines():
    lines_x = [[[(t * LINE + y) * LINE + x for x in range(LINE)] for y in range(LINE)] for t in (0, 1)]
    lines_y = [[[(t * LINE + y) * LINE + x for y in range(LINE)] for x in range(LINE)] for t in (0, 1)]
    return lines_x[0] + lines_y[1], lines_y[0] + lines_x[1]


def exchange_lines(x, lines):
    return lax.all_to_all(
        x, PLANE, split_axis=0, concat_axis=0, tiled=True, axis_index_groups=lines
    )


def on_device(
    context, out_proj, stream, norm_gain, expert_ids, slot_ids, gate_probs, w_gate, w_up, w_down
):
    core = lax.axis_index("tok").astype(jnp.int32)[None]
    turn = [(a * EXPS + b, b * EXPS + a) for a in range(HEADS) for b in range(EXPS)]
    turned = HEAD + ("exp",)
    first_lines, second_lines = plane_lines()

    got = exchange(jnp.broadcast_to(context[0], (EXPS, TOK, COLS)), "exp")

    ids, slots = expert_ids[0], slot_ids[0]
    owner = ids // EXPS
    target = jnp.where(slots >= 0, ((ids - owner * EXPS) * 2 + owner) * CAP + slots, -1)
    routes = jnp.pad(target.T.astype(F32), ((0, 0), (0, COLS - TOK)))
    stream_turned = lax.ppermute(jnp.concatenate([stream[0], routes], axis=0), turned, turn)
    own = pl.pallas_call(
        stack_kernel,
        out_shape=shape_of(3 * UNITS, WIDTH),
        in_specs=[HBM] * 3,
        out_specs=HBM,
        scratch_shapes=[pltpu.VMEM((3, UNITS, WIDTH), BF16), pltpu.SemaphoreType.DMA((6,))],
        compiler_params=pltpu.CompilerParams(vmem_limit_bytes=60 << 20),
        cost_estimate=pl.CostEstimate(flops=0, bytes_accessed=9 << 20, transcendentals=0),
    )(w_gate[0], w_up[0], w_down[0])
    got, stream_turned, own = lax.optimization_barrier((got, stream_turned, own))

    other = lax.ppermute(own, "tok", [(0, 1), (1, 0)])
    partial = call(
        project_kernel, shape_of(EXPS * TOK, COLS), [], [got.reshape(EXPS * TOK, COLS), out_proj]
    )
    parts = exchange(partial.reshape(HEADS, TOK, COLS), HEAD)
    resid_turned, picked = call(
        residual_kernel,
        (shape_of(TOK, COLS, dtype=F32), shape_of(ROWS, COLS)),
        [],
        [parts, stream_turned],
    )
    resid = lax.ppermute(resid_turned, turned, turn)
    rows = exchange(picked.reshape(EXPS, 2 * CAP, COLS), "exp")
    normed = call(
        norm_kernel,
        shape_of(LINE, 2 * CAP, WIDTH),
        [],
        [rows, norm_gain.reshape(1, WIDTH)],
    )
    line = exchange_lines(normed, first_lines)
    line, other = lax.optimization_barrier((line, other))
    forward = pl.pallas_call(
        forward_kernel,
        out_shape=shape_of(LINE, 2 * GROUP, WIDTH),
        in_specs=[SMEM, VMEM, VMEM],
        out_specs=HBM,
        scratch_shapes=[
            pltpu.VMEM((2 * GROUP, WIDTH), BF16),
            pltpu.SemaphoreType.DMA((LINE * LINE,)),
        ],
        compiler_params=pltpu.CompilerParams(vmem_limit_bytes=12 << 20),
    )(core, line.reshape(2 * GROUP, WIDTH), forward_order())
    arrived = exchange_lines(forward, second_lines)
    arrived, resid = lax.optimization_barrier((arrived, resid))
    produced = pl.pallas_call(
        expert_kernel,
        out_shape=shape_of(LINE, 2 * LINE, LINE * GROUP, COLS),
        in_specs=[SMEM, VMEM, HBM, HBM],
        out_specs=VMEM,
        scratch_shapes=[
            pltpu.VMEM((2, COLS + UNITS, WIDTH), BF16),
            pltpu.VMEM((2, UNITS, WIDTH), BF16),
            pltpu.SemaphoreType.DMA((10,)),
        ],
        compiler_params=pltpu.CompilerParams(vmem_limit_bytes=44 << 20),
        cost_estimate=pl.CostEstimate(flops=1 << 31, bytes_accessed=16 << 20, transcendentals=0),
    )(core, arrived, own, other)
    summed = call(
        add_kernel,
        shape_of(2 * LINE, LINE * GROUP, COLS),
        [],
        [exchange_lines(produced, first_lines)],
    )
    collected = call(
        collect_kernel,
        shape_of(ROWS, COLS),
        [core],
        [exchange_lines(summed.reshape(LINE, ROWS, COLS), second_lines), return_order()],
    )
    results = exchange(collected.reshape(EXPS, 2 * CAP, COLS), "exp")
    mixed = call(
        mix_kernel,
        shape_of(TOK, COLS, dtype=F32),
        [],
        [results.reshape(ROWS, COLS), target, gate_probs[0], resid],
    )
    return mixed[None]


def solution(mesh):
    split = Mesh(
        mesh.devices.reshape(mesh.shape["tok"], LINE, LINE, mesh.shape["exp"]),
        ("tok", "head_0", "head_1", "exp"),
    )
    in_specs = (
        P("exp", "tok", HEAD),
        P(HEAD, "exp"),
        P("exp", "tok", HEAD),
        P(),
        P("exp", "tok", None),
        P("exp", "tok", None),
        P("exp", "tok", None),
        P(("tok", "exp"), HEAD, None),
        P(("tok", "exp"), HEAD, None),
        P(("tok", "exp"), HEAD, None),
    )
    return jax.shard_map(
        on_device,
        mesh=split,
        in_specs=in_specs,
        out_specs=P("exp", "tok", HEAD),
        check_vma=False,
    )
```
